256 devices in a mesh: ctx: 64 (over z_hi, y, x), tp: 4 (over z_lo, core).
Axes of the slice: x: 4, y: 4, z: 8 (z_hi: 4, z_lo: 2; z = z_hi * 2 + z_lo), core: 2. Of those that a mesh axis runs over, the one named last changes fastest.
Arguments:
- q_dec: bfloat16 [2, 512, 5120], P(None, 'ctx', 'tp')
- k_dec: bfloat16 [2, 512, 5120], P(None, 'ctx', 'tp'), may hold values from -8 to 8
- v_dec: bfloat16 [2, 512, 5120], P(None, 'ctx', 'tp')
- ctx_k: bfloat16 [2, 16384, 5120], P(None, 'ctx', 'tp')
- ctx_v: bfloat16 [2, 16384, 5120], P(None, 'ctx', 'tp')
- lengths: int32 [2], replicated, may hold values from 4096 to 16384, as said below
- gain: float32 [5120], P('tp'), may hold values from 0.5 to 1.5
Outputs:
- attn_out: bfloat16 [2, 512, 5120], P(None, 'ctx', 'tp')
The draws below stay inside these ranges and needn't reach their ends.
Inputs may be any that keep to these rules, and one draw needn't show every extreme that they name: `lengths`: context positions at or past a sequence's length are unused; in every draw some sequence uses all 16384 positions.
All inputs are finite; a program needn't handle non-finite values.
Results may differ from the reference program's by a relative error of at most 0.011.
Values may be sent and summed in bfloat16 or wider, within the bound.
A program may use at most 64 MiB of HBM per device.

```python
import jax
import jax.numpy as jnp
from jax import lax

H = 40
DH = 128
HD = 5120
SEQS = 2
BLKD = 512
CTX = 16384


def head_scales(key):
    scale_key = jax.random.fold_in(key, 101)
    offset = jax.random.uniform(scale_key, (H,), dtype=jnp.float32)
    scales = 10.0 ** ((jnp.arange(H, dtype=jnp.float32) + offset) / H)
    return jnp.repeat(scales, DH)


def base_rows(key, row_index):
    row_key = jax.random.fold_in(key, 202)

    def one_row(sequence, row):
        inner = jax.random.fold_in(jax.random.fold_in(row_key, sequence), row)
        return jax.random.uniform(inner, (HD,), dtype=jnp.float32, minval=-1.7, maxval=1.7)

    def one_sequence(sequence):
        return jax.vmap(lambda row: one_row(sequence, row))(row_index)
    return jax.vmap(one_sequence)(jnp.arange(SEQS))


def target_scores(pair_index):
    return 60.0 + 60.0 * (pair_index % 4).astype(jnp.float32)


def draw_ctx_k(key, part):
    shared = key
    key = jax.random.fold_in(key, 1)
    fresh = jax.random.truncated_normal(key, -4.0, 4.0, (SEQS, CTX, HD), dtype=jnp.float32)
    pair_count = BLKD // 16
    pair_index = jnp.arange(pair_count)
    base = base_rows(shared, 2 * pair_index)
    factor = 1.0 - 2.0 / target_scores(pair_index)
    planted = jnp.stack([base, base * factor[None, :, None]], axis=2).reshape(SEQS, 2 * pair_count, HD)
    result = jnp.concatenate([planted, fresh[:, 2 * pair_count:]], axis=1)
    return result.astype(jnp.bfloat16)


def draw_q_dec(key, part):
    shared = key
    key = jax.random.fold_in(key, 2)
    fresh = jax.random.truncated_normal(key, -4.0, 4.0, (SEQS, BLKD, HD), dtype=jnp.float32)
    row_index = jnp.arange(BLKD)
    pair_index = row_index // 16
    special = row_index % 16 == 3
    rows = base_rows(shared, 2 * pair_index)
    strength = target_scores(pair_index) / (0.963 * DH ** 0.5)
    result = jnp.where(special[None, :, None], rows * strength[None, :, None], fresh)
    return result.astype(jnp.bfloat16)


def draw_ctx_v(key, part):
    scales = head_scales(key)
    key = jax.random.fold_in(key, 3)
    values = jax.random.truncated_normal(key, -4.0, 4.0, (SEQS, CTX, HD), dtype=jnp.float32)
    return (values * scales).astype(jnp.bfloat16)


def draw_v_dec(key, part):
    scales = head_scales(key)
    key = jax.random.fold_in(key, 4)
    values = jax.random.truncated_normal(key, -4.0, 4.0, (SEQS, BLKD, HD), dtype=jnp.float32)
    return (values * scales).astype(jnp.bfloat16)


def draw_lengths(key, part):
    key = jax.random.fold_in(key, 5)
    first_key, second_key = jax.random.split(key)
    drawn = jax.random.randint(first_key, (SEQS,), CTX // 4, CTX + 1, dtype=jnp.int32)
    chosen = jax.random.randint(second_key, (), 0, SEQS, dtype=jnp.int32)
    return jnp.where(jnp.arange(SEQS, dtype=jnp.int32) == chosen, CTX, drawn).astype(jnp.int32)


def levels(stream_key, extent, cuts, least, top_value):
    level, own = 1.0, jax.random.fold_in(stream_key, 6)
    for dim, shards_of in cuts:
        draws = jnp.exp(jax.random.uniform(jax.random.fold_in(own, dim), (shards_of,), jnp.float32, least / len(cuts), top_value / len(cuts)))
        level = level * jnp.repeat(draws, extent[dim] // shards_of).reshape([-1 if axis == dim else 1 for axis in range(len(extent))])
    return level


def normal_values(stream_key, extent, width, reach, pieces=(), kind=jnp.bfloat16):
    array = jax.random.normal(stream_key, extent, jnp.float32) * width
    if len(pieces) > 0:
        array = levels(stream_key, extent, pieces, -0.22, 0.18) * array
    return jnp.clip(array, min=-reach, max=reach).astype(kind)


def setup_inputs(seed: int = 0) -> dict:
    splits = jax.random.split(jax.random.key(seed), 8)
    q_dec = draw_q_dec(jax.random.fold_in(splits[7], 71), 0)
    k_dec = normal_values(splits[1], (SEQS, BLKD, HD), 2.0, 8.0, ((1, 64), (2, 4)))
    v_dec = draw_v_dec(jax.random.fold_in(splits[7], 71), 0)
    ctx_k = draw_ctx_k(jax.random.fold_in(splits[7], 71), 0)
    ctx_v = draw_ctx_v(jax.random.fold_in(splits[7], 71), 0)
    lengths = draw_lengths(jax.random.fold_in(splits[7], 71), 0)
    gain = jnp.clip(1.0 + 0.1 * jax.random.normal(splits[6], (HD,), jnp.float32), 0.5, 1.5)
    return {"q_dec": q_dec, "k_dec": k_dec, "v_dec": v_dec, "ctx_k": ctx_k, "ctx_v": ctx_v, "lengths": lengths, "gain": gain}


def reference(q_dec, k_dec, v_dec, ctx_k, ctx_v, lengths, gain):
    positions = jnp.arange(CTX, dtype=jnp.int32)
    scaling = DH ** (-0.5)
    results = []
    for sequence in range(SEQS):
        is_valid = jnp.concatenate([positions < lengths[sequence], jnp.ones((BLKD,), dtype=bool)])
        query_heads = q_dec[sequence].reshape(BLKD, H, DH).transpose(1, 0, 2)
        key_heads = jnp.concatenate([ctx_k[sequence], k_dec[sequence]], axis=0).reshape(CTX + BLKD, H, DH).transpose(1, 0, 2)
        value_heads = jnp.concatenate([ctx_v[sequence], v_dec[sequence]], axis=0).reshape(CTX + BLKD, H, DH).transpose(1, 0, 2)

        def one_head(operands):
            queries, key_rows, value_rows = operands
            scores = jnp.dot(queries, key_rows.T, preferred_element_type=jnp.float32) * scaling
            scores = jnp.where(is_valid[None, :], scores, -jnp.inf)
            row_peak = lax.optimization_barrier(jnp.max(scores, axis=1, keepdims=True))
            weights = jnp.exp(scores - row_peak)
            row_total = lax.optimization_barrier(jnp.sum(weights, axis=1, keepdims=True))
            numerator = jnp.dot(weights.astype(jnp.bfloat16), value_rows, preferred_element_type=jnp.float32)
            return numerator / row_total
        attended = lax.map(one_head, (query_heads, key_heads, value_heads))
        results.append(attended.transpose(1, 0, 2).reshape(BLKD, HD))
    attended = jnp.stack(results)
    mean_square = lax.optimization_barrier(jnp.mean(attended * attended, axis=-1, keepdims=True))
    return (attended * lax.rsqrt(mean_square + 1e-06) * gain).astype(jnp.bfloat16)
```

```python
import functools
import math

import jax
import jax.numpy as jnp
from jax import lax
from jax.experimental import pallas as pl
from jax.experimental.pallas import tpu as pltpu
from jax.sharding import PartitionSpec as P

MESH = pl.DeviceIdType.MESH
DH = 128
HEADS = 10
CHUNKS = ((0, 4), (4, 4), (8, 2))
ORDER = (("z", "y", "x"), ("z", "x", "y"), ("x", "y", "z"))
STRIDE = {"z": 16, "y": 4, "x": 1}
F32 = jnp.float32
BF16 = jnp.bfloat16
NT = (((1,), (1,)), ((), ()))


def kernel(
    q_ref, kd_ref, vd_ref, ck_ref, cv_ref, len_ref, gain_ref, out_ref,
    qbuf, sbuf, r1, s2, r2, s3, r3, st1, rs1, st2, rs2, st3, rs3, fbuf, ftbuf, nsend, nrecv,
    kbuf, vbuf, vt, kdp, vdt, bias,
    a1s, a1r, a2s, a2r, a3s, a3r, r1s, r1r, t1s, t1r, r2s, r2r, t2s, t2r, r3s, r3r, t3s, t3r, ns, nr, kvsem,
):
    ctx = lax.axis_index("ctx")
    tp = lax.axis_index("tp")
    pos = {name: (ctx // STRIDE[name]) % 4 for name in "zyx"}

    def peer(name, off):
        return (ctx + ((pos[name] + off) % 4 - pos[name]) * STRIDE[name], tp)

    kv_copies = []
    for s in range(2):
        kv_copies.append(pltpu.make_async_copy(ck_ref.at[s], kbuf.at[s], kvsem.at[0, s]))
        kv_copies.append(pltpu.make_async_copy(cv_ref.at[s], vbuf.at[s], kvsem.at[1, s]))
    for copy in kv_copies:
        copy.start()

    barrier = pltpu.get_barrier_semaphore()
    for off in (1, 2, 3):
        for name in "zyx":
            pl.semaphore_signal(barrier, inc=1, device_id=peer(name, off), device_id_type=MESH)
        pl.semaphore_signal(barrier, inc=1, device_id=(ctx, (tp + off) % 4), device_id_type=MESH)

    own = q_ref[...].astype(F32).reshape(16, HEADS * DH).astype(BF16)
    place = []
    for k, (first, count) in enumerate(CHUNKS):
        a, b, c = (pos[name] for name in ORDER[k])
        place.append((a, b, c))
        for h in range(first, first + count):
            qbuf[h, c, b, a] = own[:, h * DH : (h + 1) * DH]

    pl.semaphore_wait(barrier, 12)

    def remote(src, dst, send, recv, target):
        return pltpu.make_async_remote_copy(
            src_ref=src, dst_ref=dst, send_sem=send, recv_sem=recv, device_id=target, device_id_type=MESH
        )

    sent = []

    def a1(k, off):
        first, count = CHUNKS[k]
        a, b, c = place[k]
        block = qbuf.at[pl.ds(first, count), c, b, a]
        return remote(block, block, a1s.at[k, off - 1], a1r.at[k, off - 1], peer(ORDER[k][0], off))

    def a2(k, off):
        first, count = CHUNKS[k]
        a, b, c = place[k]
        block = qbuf.at[pl.ds(first, count), c, b]
        return remote(block, block, a2s.at[k, off - 1], a2r.at[k, off - 1], peer(ORDER[k][1], off))

    for k in range(3):
        for off in (1, 3, 2):
            copy = a1(k, off)
            copy.start()
            sent.append(copy)

    row = lax.broadcasted_iota(jnp.int32, (256, DH), 0)
    dec_row = lax.broadcasted_iota(jnp.int32, (16, DH), 0)
    for s in range(2):
        limit = len_ref[s] - ctx * 256
        bias[s, 0:256] = jnp.where(row < limit, 0.0, -jnp.inf).astype(F32)
        bias[s, 256:272] = jnp.where(dec_row < 8, 0.0, -jnp.inf).astype(F32)
        pad = jnp.zeros((8, HEADS * DH), F32)
        kdp[s] = jnp.concatenate([kd_ref[s].astype(F32), pad], axis=0).astype(BF16)
        vpad = jnp.concatenate([vd_ref[s].astype(F32), jnp.zeros((DH - 8, HEADS * DH), F32)], axis=0)
        for h in range(HEADS):
            vdt[h, s] = vpad[:, h * DH : (h + 1) * DH].T.astype(BF16)
    for k in range(3):
        for off in range(4):
            st1[k, off] = jnp.zeros((8, DH), F32)

    for copy in kv_copies:
        copy.wait()

    def wait_a1(k):
        for off in (1, 3, 2):
            a1(k, off).wait_recv()
        for off in (1, 3, 2):
            copy = a2(k, off)
            copy.start()
            sent.append(copy)

    for k in range(3):
        wait_a1(k)

    @pl.loop(0, HEADS)
    def _(h):
        lanes = pl.ds(pl.multiple_of(h * DH, DH), DH)
        for s in range(2):
            vt[h, s] = vbuf[s, :, lanes].astype(F32).T.astype(BF16)

    def a3(h, off, stride, here):
        block = qbuf.at[h, here]
        target = (ctx + ((here + off) % 4 - here) * stride, tp)
        return remote(block, block, a3s.at[h, off - 1], a3r.at[h, off - 1], target)

    for k in range(3):
        first, count = CHUNKS[k]
        for off in (1, 3, 2):
            a2(k, off).wait_recv()
        for h in range(first, first + count):
            for off in (1, 3, 2):
                a3(h, off, STRIDE[ORDER[k][2]], place[k][2]).start()

    scale = math.log2(math.e) / math.sqrt(DH)

    def attend(k, h, j, off, here):
        lanes = pl.ds(pl.multiple_of(h * DH, DH), DH)
        quarter = (here + 4 - off) % 4
        rows = qbuf[h, quarter].reshape(16, 16, DH).astype(F32)
        for s in range(2):
            q = rows[:, 8 * s : 8 * s + 8, :].reshape(DH, DH).astype(BF16)
            x0 = lax.dot_general(kbuf[s, :, lanes], q, NT, preferred_element_type=F32) * scale + bias[s, 0:256]
            x1 = lax.dot_general(kdp[s, :, lanes], q, NT, preferred_element_type=F32) * scale + bias[s, 256:272]
            peak = jnp.maximum(jnp.max(x0, axis=0, keepdims=True), jnp.max(x1, axis=0, keepdims=True))
            w0 = jnp.exp2(x0 - peak)
            w1 = jnp.exp2(x1 - peak)
            total = jnp.sum(w0, axis=0, keepdims=True) + jnp.sum(w1, axis=0, keepdims=True)
            numer = jnp.dot(vt[h, s], w0.astype(BF16), preferred_element_type=F32)
            numer += jnp.dot(vdt[h, s, :, 0:16], w1.astype(BF16), preferred_element_type=F32)
            sbuf[h, off, s] = (numer * (1.0 / total)).astype(BF16)
            st1[k, off, pl.ds(2 * j + s, 1)] = peak + jnp.log2(total)

    def r1c(h, off, stride, here):
        target = (ctx + ((here + 4 - off) % 4 - here) * stride, tp)
        return remote(sbuf.at[h, off], r1.at[h, off - 1], r1s.at[h, off - 1], r1r.at[h, off - 1], target)

    @pl.loop(0, HEADS)
    def _(t):
        k = (t % 5) % 3
        j = (t // 5) * (2 - k // 2) + (t % 5) // 3
        h = 4 * k + j
        stride = 1 + 3 * k + 9 * (k * (k - 1) // 2)
        here = (ctx // stride) % 4
        for off in (0, 1, 3, 2):
            if off:
                a3(h, off, stride, here).wait_recv()
            attend(k, h, j, off, here)
            if off:
                r1c(h, off, stride, here).start()

    def stat1(k, off):
        return remote(st1.at[k, off], rs1.at[k, off - 1], t1s.at[k, off - 1], t1r.at[k, off - 1], peer(ORDER[k][2], 4 - off))

    for k in range(3):
        for off in (1, 3, 2):
            copy = stat1(k, off)
            copy.start()
            sent.append(copy)

    def merge(parts):
        peak = functools.reduce(jnp.maximum, parts)
        weights = [jnp.exp2(part - peak) for part in parts]
        total = functools.reduce(jnp.add, weights)
        inverse = 1.0 / total
        return [w * inverse for w in weights], peak + jnp.log2(total)

    def second(k, off):
        first, count = CHUNKS[k]
        name = ORDER[k][1]
        there = (pos[name] + off) % 4
        return (
            remote(
                s2.at[there, pl.ds(first, count)], r2.at[off - 1, pl.ds(first, count)],
                r2s.at[k, off - 1], r2r.at[k, off - 1], peer(name, off),
            ),
            remote(st2.at[k], rs2.at[k, off - 1], t2s.at[k, off - 1], t2r.at[k, off - 1], peer(name, off)),
        )

    for k, (first, count) in enumerate(CHUNKS):
        for off in (1, 3, 2):
            stat1(k, off).wait_recv()
        factors, log_total = merge([st1[k, 0]] + [rs1[k, off - 1] for off in (1, 2, 3)])
        st2[k] = log_total
        for i in range(4):
            fbuf[k, i] = factors[i]

        @pl.loop(0, count)
        def _(j, k=k, first=first):
            h = first + j
            stride, here = STRIDE[ORDER[k][2]], place[k][2]
            for off in (1, 3, 2):
                r1c(h, off, stride, here).wait_recv()
            for s in range(2):
                at = pl.ds(2 * j + s, 1)
                acc = sbuf[h, 0, s].astype(F32) * fbuf[k, 0, at]
                for off in (1, 2, 3):
                    acc += r1[h, off - 1, s].astype(F32) * fbuf[k, off, at]
                rows = acc.T.astype(BF16)
                for i in range(4):
                    s2[i, h, s] = rows[32 * i : 32 * i + 32]

        for off in (1, 3, 2):
            for copy in second(k, off):
                copy.start()
                sent.append(copy)

    def third(k, off):
        first, count = CHUNKS[k]
        name = ORDER[k][0]
        there = (pos[name] + off) % 4
        return (
            remote(
                s3.at[there, pl.ds(first, count)], r3.at[off - 1, pl.ds(first, count)],
                r3s.at[k, off - 1], r3r.at[k, off - 1], peer(name, off),
            ),
            remote(st3.at[k], rs3.at[k, off - 1], t3s.at[k, off - 1], t3r.at[k, off - 1], peer(name, off)),
        )

    blank = jnp.zeros((DH - 32, DH), F32)
    for k, (first, count) in enumerate(CHUNKS):
        a, b, c = place[k]
        for off in (1, 3, 2):
            for copy in second(k, off):
                copy.wait_recv()
        factors, log_total = merge([st2[k]] + [rs2[k, off - 1] for off in (1, 2, 3)])
        st3[k] = log_total
        ftbuf[k] = jnp.concatenate(factors + [blank], axis=0).T
        fr = ftbuf[k, pl.ds(pl.multiple_of(b * 32, 32), 32)]
        for j in range(count):
            h = first + j
            merged = []
            for s in range(2):
                col = 2 * j + s
                acc = s2[b, h, s].astype(F32) * fr[:, col : col + 1]
                for off in (1, 2, 3):
                    acc += r2[off - 1, h, s].astype(F32) * fr[:, 8 * off + col : 8 * off + col + 1]
                merged.append(acc)
            for i in range(4):
                s3[i, h] = jnp.concatenate([m[8 * i : 8 * i + 8] for m in merged], axis=0).astype(BF16)
        for off in (1, 3, 2):
            for copy in third(k, off):
                copy.start()
                sent.append(copy)

    attended = []
    for k, (first, count) in enumerate(CHUNKS):
        a, b, c = place[k]
        for off in (1, 3, 2):
            for copy in third(k, off):
                copy.wait_recv()
        factors, _ = merge([st3[k]] + [rs3[k, off - 1] for off in (1, 2, 3)])
        ftbuf[3 + k] = jnp.concatenate(factors + [blank], axis=0).T
        fr = ftbuf[3 + k, pl.ds(pl.multiple_of(b * 32 + a * 8, 8), 8)]
        for j in range(count):
            h = first + j

            def column(i, j=j, fr=fr):
                return jnp.concatenate([fr[:, i * 8 + 2 * j + s : i * 8 + 2 * j + s + 1] for s in range(2)], axis=0)

            acc = s3[a, h].astype(F32) * column(0)
            for off in (1, 2, 3):
                acc += r3[off - 1, h].astype(F32) * column(off)
            attended.append(acc)

    squares = functools.reduce(jnp.add, [x * x for x in attended])
    nsend[...] = squares

    def norm(off):
        return remote(nsend, nrecv.at[off - 1], ns.at[off - 1], nr.at[off - 1], (ctx, (tp + off) % 4))

    for off in (1, 2, 3):
        copy = norm(off)
        copy.start()
        sent.append(copy)
    for off in (1, 2, 3):
        norm(off).wait_recv()
    squares = squares + nrecv[0] + nrecv[1] + nrecv[2]
    mean = jnp.sum(squares, axis=1, keepdims=True) * (1.0 / (4 * HEADS * DH))
    inverse = lax.rsqrt(mean + 1e-06)
    for h in range(HEADS):
        y = attended[h] * inverse * gain_ref[:, h * DH : (h + 1) * DH]
        for s in range(2):
            out_ref[s, :, h * DH : (h + 1) * DH] = y[8 * s : 8 * s + 8].astype(BF16)

    for copy in sent:
        copy.wait_send()
    for k, (first, count) in enumerate(CHUNKS):
        for h in range(first, first + count):
            for off in (1, 3, 2):
                a3(h, off, STRIDE[ORDER[k][2]], place[k][2]).wait_send()
                r1c(h, off, STRIDE[ORDER[k][2]], place[k][2]).wait_send()


def per_device(q_dec, k_dec, v_dec, ctx_k, ctx_v, lengths, gain):
    dma = pltpu.SemaphoreType.DMA
    vmem = pl.BlockSpec(memory_space=pltpu.VMEM)
    hbm = pl.BlockSpec(memory_space=pl.ANY)
    scratch = [
        pltpu.VMEM((HEADS, 4, 4, 4, 16, DH), BF16),
        pltpu.VMEM((HEADS, 4, 2, DH, DH), BF16),
        pltpu.VMEM((HEADS, 3, 2, DH, DH), BF16),
        pltpu.VMEM((4, HEADS, 2, 32, DH), BF16),
        pltpu.VMEM((3, HEADS, 2, 32, DH), BF16),
        pltpu.VMEM((4, HEADS, 16, DH), BF16),
        pltpu.VMEM((3, HEADS, 16, DH), BF16),
        pltpu.VMEM((3, 4, 8, DH), F32),
        pltpu.VMEM((3, 3, 8, DH), F32),
        pltpu.VMEM((3, 8, DH), F32),
        pltpu.VMEM((3, 3, 8, DH), F32),
        pltpu.VMEM((3, 8, DH), F32),
        pltpu.VMEM((3, 3, 8, DH), F32),
        pltpu.VMEM((3, 4, 8, DH), F32),
        pltpu.VMEM((6, DH, DH), F32),
        pltpu.VMEM((16, DH), F32),
        pltpu.VMEM((3, 16, DH), F32),
        pltpu.VMEM((2, 256, HEADS * DH), BF16),
        pltpu.VMEM((2, 256, HEADS * DH), BF16),
        pltpu.VMEM((HEADS, 2, DH, 256), BF16),
        pltpu.VMEM((2, 16, HEADS * DH), BF16),
        pltpu.VMEM((HEADS, 2, DH, DH), BF16),
        pltpu.VMEM((2, 272, DH), F32),
        dma((3, 3)), dma((3, 3)), dma((3, 3)), dma((3, 3)),
        dma((HEADS, 3)), dma((HEADS, 3)), dma((HEADS, 3)), dma((HEADS, 3)),
        dma((3, 3)), dma((3, 3)), dma((3, 3)), dma((3, 3)), dma((3, 3)), dma((3, 3)),
        dma((3, 3)), dma((3, 3)), dma((3, 3)), dma((3, 3)),
        dma((3,)), dma((3,)),
        dma((2, 2)),
    ]
    return pl.pallas_call(
        kernel,
        out_shape=jax.ShapeDtypeStruct(q_dec.shape, BF16),
        in_specs=[vmem, vmem, vmem, hbm, hbm, pl.BlockSpec(memory_space=pltpu.SMEM), vmem],
        out_specs=vmem,
        scratch_shapes=scratch,
        compiler_params=pltpu.CompilerParams(
            collective_id=0, has_side_effects=True, vmem_limit_bytes=48 << 20
        ),
        cost_estimate=pl.CostEstimate(flops=1_400_000_000, bytes_accessed=8_000_000, transcendentals=2_700_000),
        name="block_attention",
    )(q_dec, k_dec, v_dec, ctx_k, ctx_v, lengths, gain.reshape(1, -1))


def solution(mesh):
    return jax.shard_map(
        per_device,
        mesh=mesh,
        in_specs=(
            P(None, "ctx", "tp"),
            P(None, "ctx", "tp"),
            P(None, "ctx", "tp"),
            P(None, "ctx", "tp"),
            P(None, "ctx", "tp"),
            P(),
            P("tp"),
        ),
        out_specs=P(None, "ctx", "tp"),
        check_vma=False,
    )
```

```python
import functools
import math

import jax
import jax.numpy as jnp
from jax import lax
from jax.experimental import pallas as pl
from jax.experimental.pallas import tpu as pltpu
from jax.sharding import PartitionSpec as P

MESH = pl.DeviceIdType.MESH
DH = 128
HEADS = 10
CHUNKS = ((0, 4), (4, 4), (8, 2))
ORDER = (("z", "y", "x"), ("z", "x", "y"), ("x", "y", "z"))
STRIDE = {"z": 16, "y": 4, "x": 1}
F32 = jnp.float32
BF16 = jnp.bfloat16
NT = (((1,), (1,)), ((), ()))
OFFS = (1, 3, 2)
LAG1, LAG2, LAG3 = 2, 4, 6


def kernel(
    q_hbm, kd_hbm, vd_hbm, ck_hbm, cv_hbm, len_hbm, gain_hbm, out_ref,
    q_ref, kd_ref, vd_ref, kbuf, vbuf, len_ref, gain_ref,
    qbuf, s1, r1, s2, r2, s3, r3, factor, attended, nsend, nrecv, vt, kdp, vdt, bias,
    insem, a1s, a1r, a2s, a2r, a3s, a3r, r1s, r1r, r2s, r2r, r3s, r3r, ns, nr,
):
    ctx = lax.axis_index("ctx")
    tp = lax.axis_index("tp")
    pos = {name: (ctx // STRIDE[name]) % 4 for name in "zyx"}

    loads = [
        pltpu.make_async_copy(src, dst, insem.at[i])
        for i, (src, dst) in enumerate((
            (q_hbm, q_ref), (kd_hbm, kd_ref), (vd_hbm, vd_ref), (ck_hbm, kbuf), (cv_hbm, vbuf), (len_hbm, len_ref), (gain_hbm, gain_ref),
        ))
    ]
    for load in loads:
        load.start()

    def along(stride, off):
        here = (ctx // stride) % 4
        return (ctx + ((here + off) % 4 - here) * stride, tp)

    barrier = pltpu.get_barrier_semaphore()
    for off in (1, 2, 3):
        for name in "zyx":
            pl.semaphore_signal(barrier, inc=1, device_id=along(STRIDE[name], off), device_id_type=MESH)
        pl.semaphore_signal(barrier, inc=1, device_id=(ctx, (tp + off) % 4), device_id_type=MESH)

    loads[0].wait()
    own = q_ref[...].astype(F32).reshape(16, HEADS * DH).astype(BF16)
    place = []
    for k, (first, count) in enumerate(CHUNKS):
        a, b, c = (pos[name] for name in ORDER[k])
        place.append((a, b, c))
        for h in range(first, first + count):
            qbuf[h, c, b, a] = own[:, h * DH : (h + 1) * DH]

    pl.semaphore_wait(barrier, 12)

    def remote(src, dst, send, recv, target):
        return pltpu.make_async_remote_copy(
            src_ref=src, dst_ref=dst, send_sem=send, recv_sem=recv, device_id=target, device_id_type=MESH
        )

    def a1(k, off):
        first, count = CHUNKS[k]
        a, b, c = place[k]
        block = qbuf.at[pl.ds(first, count), c, b, a]
        return remote(block, block, a1s.at[k, off - 1], a1r.at[k, off - 1], along(STRIDE[ORDER[k][0]], off))

    def a2(k, off):
        first, count = CHUNKS[k]
        a, b, c = place[k]
        block = qbuf.at[pl.ds(first, count), c, b]
        return remote(block, block, a2s.at[k, off - 1], a2r.at[k, off - 1], along(STRIDE[ORDER[k][1]], off))

    for k in (2, 0, 1):
        for off in OFFS:
            a1(k, off).start()

    for load in loads[1:]:
        load.wait()
    row = lax.broadcasted_iota(jnp.int32, (256, DH), 0)
    dec_row = lax.broadcasted_iota(jnp.int32, (16, DH), 0)
    for s in range(2):
        limit = len_ref[s] - ctx * 256
        bias[s, 0:256] = jnp.where(row < limit, 0.0, -jnp.inf).astype(F32)
        bias[s, 256:272] = jnp.where(dec_row < 8, 0.0, -jnp.inf).astype(F32)
        pad = jnp.zeros((8, HEADS * DH), F32)
        kdp[s] = jnp.concatenate([kd_ref[s].astype(F32), pad], axis=0).astype(BF16)
        vpad = jnp.concatenate([vd_ref[s].astype(F32), jnp.zeros((DH - 8, HEADS * DH), F32)], axis=0)
        for h in range(HEADS):
            vdt[h, s] = vpad[:, h * DH : (h + 1) * DH].T.astype(BF16)

    for k in (2, 0, 1):
        for off in OFFS:
            a1(k, off).wait_recv()
        for off in OFFS:
            a2(k, off).start()

    @pl.loop(0, HEADS)
    def _(h):
        lanes = pl.ds(pl.multiple_of(h * DH, DH), DH)
        for s in range(2):
            vt[h, s] = vbuf[s, :, lanes].astype(F32).T.astype(BF16)

    def head_of(t):
        k = (t % 5) % 3
        return 4 * k + (t // 5) * (2 - k // 2) + (t % 5) // 3, k

    def stride_a(k):
        return 16 - 15 * (k * (k - 1) // 2)

    def stride_b(k):
        return 4 - 3 * (k * (2 - k))

    def stride_c(k):
        return 1 + 3 * k + 9 * (k * (k - 1) // 2)

    def a3(h, k, off):
        block = qbuf.at[h, (ctx // stride_c(k)) % 4]
        return remote(block, block, a3s.at[h, off - 1], a3r.at[h, off - 1], along(stride_c(k), off))

    def first_back(h, k, off):
        return remote(s1.at[h, off], r1.at[h, off - 1], r1s.at[h, off - 1], r1r.at[h, off - 1], along(stride_c(k), 4 - off))

    def second_back(h, k, off):
        there = ((ctx // stride_b(k)) % 4 + off) % 4
        return remote(s2.at[h, there], r2.at[h, off - 1], r2s.at[h, off - 1], r2r.at[h, off - 1], along(stride_b(k), off))

    def third_back(h, k, off):
        there = ((ctx // stride_a(k)) % 4 + off) % 4
        return remote(s3.at[h, there], r3.at[h, off - 1], r3s.at[h, off - 1], r3r.at[h, off - 1], along(stride_a(k), off))

    for k in (2, 0, 1):
        first, count = CHUNKS[k]
        for off in OFFS:
            a2(k, off).wait_recv()
        for h in range(first, first + count):
            for off in OFFS:
                a3(h, k, off).start()

    scale = math.log2(math.e) / math.sqrt(DH)

    def split(lse):
        high = lse.astype(BF16).astype(F32)
        middle = (lse - high).astype(BF16).astype(F32)
        low = lse - high - middle
        return jnp.concatenate([high, middle, low, jnp.zeros((10, DH), F32)], axis=0).astype(BF16)

    def join(block):
        rows = block.astype(F32)
        return rows[0:2] + rows[2:4] + rows[4:6]

    def attend(h, k, offs):
        lanes = pl.ds(pl.multiple_of(h * DH, DH), DH)
        here = (ctx // stride_c(k)) % 4
        rows = [qbuf[h, (here + 4 - off) % 4].reshape(16, 16, DH).astype(F32) for off in offs]
        lse = []
        for s in range(2):
            q = jnp.concatenate([x[:, 8 * s : 8 * s + 8, :].reshape(DH, DH) for x in rows], axis=0).astype(BF16)
            edge = jnp.concatenate([bias[s]] * 2, axis=1)
            x0 = lax.dot_general(kbuf[s, :, lanes], q, NT, preferred_element_type=F32) * scale + edge[0:256]
            x1 = lax.dot_general(kdp[s, :, lanes], q, NT, preferred_element_type=F32) * scale + edge[256:272]
            peak = jnp.maximum(jnp.max(x0, axis=0, keepdims=True), jnp.max(x1, axis=0, keepdims=True))
            w0 = jnp.exp2(x0 - peak)
            w1 = jnp.exp2(x1 - peak)
            total = jnp.sum(w0, axis=0, keepdims=True) + jnp.sum(w1, axis=0, keepdims=True)
            numer = jnp.dot(vt[h, s], w0.astype(BF16), preferred_element_type=F32)
            numer += jnp.dot(vdt[h, s, :, 0:16], w1.astype(BF16), preferred_element_type=F32)
            part = (numer * (1.0 / total)).astype(BF16)
            lse.append(peak + jnp.log2(total))
            for i, off in enumerate(offs):
                s1[h, off, DH * s : DH * s + DH] = part[:, DH * i : DH * i + DH]
        for i, off in enumerate(offs):
            s1[h, off, 256:272] = split(jnp.concatenate([x[:, DH * i : DH * i + DH] for x in lse], axis=0))

    def merge(parts):
        peak = functools.reduce(jnp.maximum, parts)
        weights = [jnp.exp2(part - peak) for part in parts]
        total = functools.reduce(jnp.add, weights)
        inverse = 1.0 / total
        return [w * inverse for w in weights], peak + jnp.log2(total)

    def turned(factors):
        return jnp.concatenate(factors + [jnp.zeros((DH - 8, DH), F32)], axis=0).T

    def merge_first(h, k):
        for off in OFFS:
            first_back(h, k, off).wait_recv()
        parts = [s1.at[h, 0]] + [r1.at[h, off - 1] for off in (1, 2, 3)]
        factors, lse = merge([join(part[256:272]) for part in parts])
        tail = split(lse)
        for s in range(2):
            acc = parts[0][DH * s : DH * s + DH].astype(F32) * factors[0][s : s + 1]
            for i in (1, 2, 3):
                acc += parts[i][DH * s : DH * s + DH].astype(F32) * factors[i][s : s + 1]
            rows = acc.T.astype(BF16)
            for i in range(4):
                s2[h, i, 32 * s : 32 * s + 32] = rows[32 * i : 32 * i + 32]
        for i in range(4):
            s2[h, i, 64:80] = tail
        for off in OFFS:
            second_back(h, k, off).start()

    def merge_second(h, k):
        b = (ctx // stride_b(k)) % 4
        for off in OFFS:
            second_back(h, k, off).wait_recv()
        parts = [s2.at[h, b]] + [r2.at[h, off - 1] for off in (1, 2, 3)]
        factors, lse = merge([join(part[64:80]) for part in parts])
        tail = split(lse)
        factor[0] = turned(factors)
        columns = factor[0, pl.ds(pl.multiple_of(b * 32, 32), 32)]
        merged = []
        for s in range(2):
            acc = parts[0][32 * s : 32 * s + 32].astype(F32) * columns[:, s : s + 1]
            for i in (1, 2, 3):
                acc += parts[i][32 * s : 32 * s + 32].astype(F32) * columns[:, 2 * i + s : 2 * i + s + 1]
            merged.append(acc)
        for i in range(4):
            s3[h, i, 0:16] = jnp.concatenate([m[8 * i : 8 * i + 8] for m in merged], axis=0).astype(BF16)
            s3[h, i, 16:32] = tail
        for off in OFFS:
            third_back(h, k, off).start()

    def merge_third(h, k):
        a = (ctx // stride_a(k)) % 4
        b = (ctx // stride_b(k)) % 4
        for off in OFFS:
            third_back(h, k, off).wait_recv()
        parts = [s3.at[h, a]] + [r3.at[h, off - 1] for off in (1, 2, 3)]
        factors, _ = merge([join(part[16:32]) for part in parts])
        factor[1] = turned(factors)
        columns = factor[1, pl.ds(pl.multiple_of(b * 32 + a * 8, 8), 8)]
        acc = jnp.zeros((16, DH), F32)
        for i in range(4):
            column = jnp.concatenate([columns[:, 2 * i + s : 2 * i + s + 1] for s in range(2)], axis=0)
            acc += parts[i][0:16].astype(F32) * column
        attended[h] = acc

    @pl.loop(0, HEADS + LAG3)
    def _(t):
        @pl.when(t < HEADS)
        def _():
            h, k = head_of(t)
            a3(h, k, 1).wait_recv()
            attend(h, k, (0, 1))
            first_back(h, k, 1).start()
            a3(h, k, 3).wait_recv()
            a3(h, k, 2).wait_recv()
            attend(h, k, (3, 2))
            first_back(h, k, 3).start()
            first_back(h, k, 2).start()

        @pl.when((t >= LAG1) & (t < HEADS + LAG1))
        def _():
            merge_first(*head_of(t - LAG1))

        @pl.when((t >= LAG2) & (t < HEADS + LAG2))
        def _():
            merge_second(*head_of(t - LAG2))

        @pl.when(t >= LAG3)
        def _():
            merge_third(*head_of(t - LAG3))

    squares = attended[0] * attended[0]
    for h in range(1, HEADS):
        squares += attended[h] * attended[h]
    nsend[...] = squares

    def norm(off):
        return remote(nsend, nrecv.at[off - 1], ns.at[off - 1], nr.at[off - 1], (ctx, (tp + off) % 4))

    for off in (1, 2, 3):
        norm(off).start()

    for k in range(3):
        for off in OFFS:
            a1(k, off).wait_send()
            a2(k, off).wait_send()

    @pl.loop(0, HEADS)
    def _(t):
        h, k = head_of(t)
        for off in OFFS:
            a3(h, k, off).wait_send()
            first_back(h, k, off).wait_send()
            second_back(h, k, off).wait_send()
            third_back(h, k, off).wait_send()

    for off in (1, 2, 3):
        norm(off).wait()
    squares = squares + nrecv[0] + nrecv[1] + nrecv[2]
    mean = jnp.sum(squares, axis=1, keepdims=True) * (1.0 / (4 * HEADS * DH))
    inverse = lax.rsqrt(mean + 1e-06)
    for h in range(HEADS):
        y = attended[h] * inverse * gain_ref[h * DH : (h + 1) * DH].reshape(1, DH)
        for s in range(2):
            out_ref[s, :, h * DH : (h + 1) * DH] = y[8 * s : 8 * s + 8].astype(BF16)


def per_device(q_dec, k_dec, v_dec, ctx_k, ctx_v, lengths, gain):
    dma = pltpu.SemaphoreType.DMA
    hbm = pl.BlockSpec(memory_space=pltpu.HBM)
    scratch = [
        pltpu.VMEM((2, 8, HEADS * DH), BF16),
        pltpu.VMEM((2, 8, HEADS * DH), BF16),
        pltpu.VMEM((2, 8, HEADS * DH), BF16),
        pltpu.VMEM((2, 256, HEADS * DH), BF16),
        pltpu.VMEM((2, 256, HEADS * DH), BF16),
        pltpu.SMEM((2,), jnp.int32),
        pltpu.VMEM((HEADS * DH,), F32),
        pltpu.VMEM((HEADS, 4, 4, 4, 16, DH), BF16),
        pltpu.VMEM((HEADS, 4, 272, DH), BF16),
        pltpu.VMEM((HEADS, 3, 272, DH), BF16),
        pltpu.VMEM((HEADS, 4, 80, DH), BF16),
        pltpu.VMEM((HEADS, 3, 80, DH), BF16),
        pltpu.VMEM((HEADS, 4, 32, DH), BF16),
        pltpu.VMEM((HEADS, 3, 32, DH), BF16),
        pltpu.VMEM((2, DH, DH), F32),
        pltpu.VMEM((HEADS, 16, DH), F32),
        pltpu.VMEM((16, DH), F32),
        pltpu.VMEM((3, 16, DH), F32),
        pltpu.VMEM((HEADS, 2, DH, 256), BF16),
        pltpu.VMEM((2, 16, HEADS * DH), BF16),
        pltpu.VMEM((HEADS, 2, DH, DH), BF16),
        pltpu.VMEM((2, 272, DH), F32),
        dma((7,)),
        dma((3, 3)), dma((3, 3)), dma((3, 3)), dma((3, 3)),
        dma((HEADS, 3)), dma((HEADS, 3)), dma((HEADS, 3)), dma((HEADS, 3)),
        dma((HEADS, 3)), dma((HEADS, 3)), dma((HEADS, 3)), dma((HEADS, 3)),
        dma((3,)), dma((3,)),
    ]
    return pl.pallas_call(
        kernel,
        out_shape=jax.ShapeDtypeStruct(q_dec.shape, BF16),
        in_specs=[hbm] * 7,
        out_specs=pl.BlockSpec(memory_space=pltpu.VMEM),
        scratch_shapes=scratch,
        compiler_params=pltpu.CompilerParams(
            collective_id=0, has_side_effects=True, vmem_limit_bytes=62 << 20
        ),
        cost_estimate=pl.CostEstimate(flops=1_400_000_000, bytes_accessed=8_000_000, transcendentals=2_700_000),
        name="block_attention",
    )(q_dec, k_dec, v_dec, ctx_k, ctx_v, lengths, gain)


def solution(mesh):
    return jax.shard_map(
        per_device,
        mesh=mesh,
        in_specs=(
            P(None, "ctx", "tp"),
            P(None, "ctx", "tp"),
            P(None, "ctx", "tp"),
            P(None, "ctx", "tp"),
            P(None, "ctx", "tp"),
            P(),
            P("tp"),
        ),
        out_specs=P(None, "ctx", "tp"),
        check_vma=False,
    )
```

```python
import functools
import math

import jax
import jax.numpy as jnp
from jax import lax
from jax.experimental import pallas as pl
from jax.experimental.pallas import tpu as pltpu
from jax.sharding import PartitionSpec as P

MESH = pl.DeviceIdType.MESH
DH = 128
HEADS = 10
CHUNKS = ((0, 4), (4, 4), (8, 2))
ORDER = (("z", "y", "x"), ("z", "x", "y"), ("x", "y", "z"))
STRIDE = {"z": 16, "y": 4, "x": 1}
F32 = jnp.float32
BF16 = jnp.bfloat16
NT = (((1,), (1,)), ((), ()))
OFFS = (1, 3, 2)
LAG1, LAG2 = 4, 8


def kernel(
    q_hbm, kd_hbm, vd_hbm, ck_hbm, cv_hbm, len_hbm, gain_hbm, out_ref,
    q_ref, kd_ref, vd_ref, kbuf, vbuf, len_ref, gain_ref,
    qbuf, s1, r1, s2, r2, s3, r3, attended, nsend, nrecv, vt, kdp, vdt, bias,
    insem, g0s, g0r, g1s, g1r, g2s, g2r, g3s, g3r, r1s, r1r, r2s, r2r, r3s, r3r, ns, nr,
):
    ctx = lax.axis_index("ctx")
    tp = lax.axis_index("tp")
    loads = [
        pltpu.make_async_copy(src, dst, insem.at[i])
        for i, (src, dst) in enumerate((
            (q_hbm, q_ref), (kd_hbm, kd_ref), (vd_hbm, vd_ref), (ck_hbm, kbuf), (cv_hbm, vbuf), (len_hbm, len_ref), (gain_hbm, gain_ref),
        ))
    ]
    for load in loads:
        load.start()

    def along(stride, off):
        here = (ctx // stride) % 4
        return (ctx + ((here + off) % 4 - here) * stride, tp)

    barrier = pltpu.get_barrier_semaphore()
    for off in (1, 2, 3):
        for name in "zyx":
            pl.semaphore_signal(barrier, inc=1, device_id=along(STRIDE[name], off), device_id_type=MESH)
        pl.semaphore_signal(barrier, inc=1, device_id=(ctx, (tp + off) % 4), device_id_type=MESH)

    loads[0].wait()
    own = q_ref[...].astype(F32).reshape(16, HEADS * DH).astype(BF16)
    for h in range(HEADS):
        qbuf[h, 0, 0, 0] = own[:, h * DH : (h + 1) * DH]

    pl.semaphore_wait(barrier, 12)

    def remote(src, dst, send, recv, target):
        return pltpu.make_async_remote_copy(
            src_ref=src, dst_ref=dst, send_sem=send, recv_sem=recv, device_id=target, device_id_type=MESH
        )

    def heads(k):
        return pl.ds(CHUNKS[k][0], CHUNKS[k][1])

    def own_block(k, axis, off):
        spot = [0, 0, 0]
        spot[2 - axis] = off
        return remote(
            qbuf.at[heads(k), 0, 0, 0], qbuf.at[heads(k), spot[0], spot[1], spot[2]],
            g0s.at[k, axis, off - 1], g0r.at[k, axis, off - 1], along(STRIDE[ORDER[k][axis]], off),
        )

    def a_to_b(k, hop, off):
        return remote(
            qbuf.at[heads(k), 0, 0, hop], qbuf.at[heads(k), 0, off, hop],
            g1s.at[k, hop - 1, off - 1], g1r.at[k, hop - 1, off - 1], along(STRIDE[ORDER[k][1]], off),
        )

    def a_to_c(k, off):
        return remote(
            qbuf.at[heads(k), 0, 0, pl.ds(1, 3)], qbuf.at[heads(k), off, 0, pl.ds(1, 3)],
            g2s.at[k, 0, off - 1], g2r.at[k, 0, off - 1], along(STRIDE[ORDER[k][2]], off),
        )

    def b_to_c(k, off):
        return remote(
            qbuf.at[heads(k), 0, pl.ds(1, 3), 0], qbuf.at[heads(k), off, pl.ds(1, 3), 0],
            g2s.at[k, 1, off - 1], g2r.at[k, 1, off - 1], along(STRIDE[ORDER[k][2]], off),
        )

    for k in (2, 0, 1):
        for off in OFFS:
            own_block(k, 0, off).start()
    for axis in (1, 2):
        for k in (2, 0, 1):
            for off in OFFS:
                own_block(k, axis, off).start()

    for load in loads[1:]:
        load.wait()
    row = lax.broadcasted_iota(jnp.int32, (256, DH), 0)
    dec_row = lax.broadcasted_iota(jnp.int32, (16, DH), 0)
    for s in range(2):
        limit = len_ref[s] - ctx * 256
        bias[s, 0:256] = jnp.where(row < limit, 0.0, -jnp.inf).astype(F32)
        bias[s, 256:272] = jnp.where(dec_row < 8, 0.0, -jnp.inf).astype(F32)
        pad = jnp.zeros((8, HEADS * DH), F32)
        kdp[s] = jnp.concatenate([kd_ref[s].astype(F32), pad], axis=0).astype(BF16)
        vpad = jnp.concatenate([vd_ref[s].astype(F32), jnp.zeros((DH - 8, HEADS * DH), F32)], axis=0)
        for h in range(HEADS):
            vdt[h, s] = vpad[:, h * DH : (h + 1) * DH].T.astype(BF16)

    for hop in OFFS:
        for k in (2, 0, 1):
            own_block(k, 0, hop).wait_recv()
            for off in OFFS:
                a_to_b(k, hop, off).start()
    for k in (2, 0, 1):
        for off in OFFS:
            a_to_c(k, off).start()
        for off in OFFS:
            own_block(k, 1, off).wait_recv()
        for off in OFFS:
            b_to_c(k, off).start()

    @pl.loop(0, HEADS)
    def _(h):
        lanes = pl.ds(pl.multiple_of(h * DH, DH), DH)
        for s in range(2):
            vt[h, s] = vbuf[s, :, lanes].astype(F32).T.astype(BF16)

    def head_of(t):
        k = (t % 5) % 3
        return 4 * k + (t // 5) * (2 - k // 2) + (t % 5) // 3, k

    def stride_a(k):
        return 16 - 15 * (k * (k - 1) // 2)

    def stride_b(k):
        return 4 - 3 * (k * (2 - k))

    def stride_c(k):
        return 1 + 3 * k + 9 * (k * (k - 1) // 2)

    def ab_to_c(h, k, off):
        return remote(
            qbuf.at[h, 0, pl.ds(1, 3), pl.ds(1, 3)], qbuf.at[h, off, pl.ds(1, 3), pl.ds(1, 3)],
            g3s.at[h, off - 1], g3r.at[h, off - 1], along(stride_c(k), off),
        )

    def first_back(h, k, off):
        return remote(s1.at[h, off], r1.at[h, off - 1], r1s.at[h, off - 1], r1r.at[h, off - 1], along(stride_c(k), 4 - off))

    def second_back(h, k, off):
        return remote(s2.at[h, off], r2.at[h, off - 1], r2s.at[h, off - 1], r2r.at[h, off - 1], along(stride_b(k), 4 - off))

    def third_back(h, k, off):
        return remote(s3.at[h, off], r3.at[h, off - 1], r3s.at[h, off - 1], r3r.at[h, off - 1], along(stride_a(k), 4 - off))

    for k in (2, 0, 1):
        first, count = CHUNKS[k]
        for hop in OFFS:
            for off in OFFS:
                a_to_b(k, hop, off).wait_recv()
        for h in range(first, first + count):
            for off in OFFS:
                ab_to_c(h, k, off).start()
    for k in (2, 0, 1):
        for off in OFFS:
            own_block(k, 2, off).wait_recv()
            a_to_c(k, off).wait_recv()
            b_to_c(k, off).wait_recv()

    scale = math.log2(math.e) / math.sqrt(DH)

    def split(lse):
        high = lse.astype(BF16).astype(F32)
        middle = (lse - high).astype(BF16).astype(F32)
        low = lse - high - middle
        return jnp.concatenate([high, middle, low, jnp.zeros((10, DH), F32)], axis=0).astype(BF16)

    def join(block):
        rows = block.astype(F32)
        return rows[0:2] + rows[2:4] + rows[4:6]

    def attend(h, offs):
        lanes = pl.ds(pl.multiple_of(h * DH, DH), DH)
        rows = [qbuf[h, off].reshape(16, 16, DH).astype(F32) for off in offs]
        lse = []
        for s in range(2):
            q = jnp.concatenate([x[:, 8 * s : 8 * s + 8, :].reshape(DH, DH) for x in rows], axis=0).astype(BF16)
            edge = jnp.concatenate([bias[s]] * 2, axis=1)
            x0 = lax.dot_general(kbuf[s, :, lanes], q, NT, preferred_element_type=F32) * scale + edge[0:256]
            x1 = lax.dot_general(kdp[s, :, lanes], q, NT, preferred_element_type=F32) * scale + edge[256:272]
            peak = jnp.maximum(jnp.max(x0, axis=0, keepdims=True), jnp.max(x1, axis=0, keepdims=True))
            w0 = jnp.exp2(x0 - peak)
            w1 = jnp.exp2(x1 - peak)
            total = jnp.sum(w0, axis=0, keepdims=True) + jnp.sum(w1, axis=0, keepdims=True)
            numer = jnp.dot(vt[h, s], w0.astype(BF16), preferred_element_type=F32)
            numer += jnp.dot(vdt[h, s, :, 0:16], w1.astype(BF16), preferred_element_type=F32)
            part = (numer * (1.0 / total)).astype(BF16)
            lse.append(peak + jnp.log2(total))
            for i, off in enumerate(offs):
                s1[h, off, DH * s : DH * s + DH] = part[:, DH * i : DH * i + DH]
        for i, off in enumerate(offs):
            s1[h, off, 256:272] = split(jnp.concatenate([x[:, DH * i : DH * i + DH] for x in lse], axis=0))

    def merge(parts):
        peak = functools.reduce(jnp.maximum, parts)
        weights = [jnp.exp2(part - peak) for part in parts]
        total = functools.reduce(jnp.add, weights)
        inverse = 1.0 / total
        return [w * inverse for w in weights], peak + jnp.log2(total)

    def shifted(rows, lanes):
        return pltpu.roll(rows, DH - lanes, 1) if lanes else rows

    def turned(factors):
        return jnp.concatenate(factors + [jnp.zeros((DH - 8, DH), F32)], axis=0).T

    def merge_first(h, k):
        for off in OFFS:
            first_back(h, k, off).wait_recv()
        parts = [s1.at[h, 0]] + [r1.at[h, off - 1] for off in (1, 2, 3)]
        factors, lse = merge([join(part[256:272]) for part in parts])
        tail = split(lse)
        for s in range(2):
            acc = parts[0][DH * s : DH * s + DH].astype(F32) * factors[0][s : s + 1]
            for i in (1, 2, 3):
                acc += parts[i][DH * s : DH * s + DH].astype(F32) * factors[i][s : s + 1]
            rows = acc.T.astype(BF16)
            for i in range(4):
                s2[h, i, 32 * s : 32 * s + 32] = rows[32 * i : 32 * i + 32]
        for i in range(4):
            s2[h, i, 64:80] = tail
        for off in OFFS:
            second_back(h, k, off).start()

    def merge_second(h, k):
        for off in OFFS:
            second_back(h, k, off).wait_recv()
        parts = [s2.at[h, 0]] + [r2.at[h, off - 1] for off in (1, 2, 3)]
        factors, lse = merge([shifted(join(part[64:80]), 32 * i) for i, part in enumerate(parts)])
        tail = split(lse)
        columns = turned(factors)[0:32]
        merged = []
        for s in range(2):
            acc = parts[0][32 * s : 32 * s + 32].astype(F32) * columns[:, s : s + 1]
            for i in (1, 2, 3):
                acc += parts[i][32 * s : 32 * s + 32].astype(F32) * columns[:, 2 * i + s : 2 * i + s + 1]
            merged.append(acc)
        for i in range(4):
            s3[h, i, 0:16] = jnp.concatenate([m[8 * i : 8 * i + 8] for m in merged], axis=0).astype(BF16)
            s3[h, i, 16:32] = tail
        for off in OFFS:
            third_back(h, k, off).start()

    def merge_third(h, k):
        for off in OFFS:
            third_back(h, k, off).wait_recv()
        parts = [s3.at[h, 0]] + [r3.at[h, off - 1] for off in (1, 2, 3)]
        factors, _ = merge([shifted(join(part[16:32]), 8 * i) for i, part in enumerate(parts)])
        columns = turned(factors)[0:8]
        acc = jnp.zeros((16, DH), F32)
        for i in range(4):
            column = jnp.concatenate([columns[:, 2 * i + s : 2 * i + s + 1] for s in range(2)], axis=0)
            acc += parts[i][0:16].astype(F32) * column
        attended[h] = acc

    @pl.loop(0, HEADS)
    def _(t):
        h, k = head_of(t)
        ab_to_c(h, k, 1).wait_recv()
        attend(h, (0, 1))
        first_back(h, k, 1).start()
        ab_to_c(h, k, 3).wait_recv()
        ab_to_c(h, k, 2).wait_recv()
        attend(h, (3, 2))
        first_back(h, k, 3).start()
        first_back(h, k, 2).start()

        @pl.when(t >= LAG1)
        def _():
            merge_first(*head_of(t - LAG1))

        @pl.when(t >= LAG2)
        def _():
            merge_second(*head_of(t - LAG2))

    @pl.loop(HEADS - LAG1, HEADS)
    def _(t):
        merge_first(*head_of(t))

    @pl.loop(HEADS - LAG2, HEADS)
    def _(t):
        merge_second(*head_of(t))

    @pl.loop(0, HEADS)
    def _(t):
        merge_third(*head_of(t))

    squares = attended[0] * attended[0]
    for h in range(1, HEADS):
        squares += attended[h] * attended[h]
    nsend[...] = squares

    def norm(off):
        return remote(nsend, nrecv.at[off - 1], ns.at[off - 1], nr.at[off - 1], (ctx, (tp + off) % 4))

    for off in (1, 2, 3):
        norm(off).start()

    for k in range(3):
        for off in OFFS:
            for axis in range(3):
                own_block(k, axis, off).wait_send()
            for hop in OFFS:
                a_to_b(k, hop, off).wait_send()
            a_to_c(k, off).wait_send()
            b_to_c(k, off).wait_send()

    @pl.loop(0, HEADS)
    def _(t):
        h, k = head_of(t)
        for off in OFFS:
            ab_to_c(h, k, off).wait_send()
            first_back(h, k, off).wait_send()
            second_back(h, k, off).wait_send()
            third_back(h, k, off).wait_send()

    for off in (1, 2, 3):
        norm(off).wait()
    squares = squares + nrecv[0] + nrecv[1] + nrecv[2]
    mean = jnp.sum(squares, axis=1, keepdims=True) * (1.0 / (4 * HEADS * DH))
    inverse = lax.rsqrt(mean + 1e-06)
    for h in range(HEADS):
        y = attended[h] * inverse * gain_ref[h * DH : (h + 1) * DH].reshape(1, DH)
        for s in range(2):
            out_ref[s, :, h * DH : (h + 1) * DH] = y[8 * s : 8 * s + 8].astype(BF16)


def per_device(q_dec, k_dec, v_dec, ctx_k, ctx_v, lengths, gain):
    dma = pltpu.SemaphoreType.DMA
    hbm = pl.BlockSpec(memory_space=pltpu.HBM)
    scratch = [
        pltpu.VMEM((2, 8, HEADS * DH), BF16),
        pltpu.VMEM((2, 8, HEADS * DH), BF16),
        pltpu.VMEM((2, 8, HEADS * DH), BF16),
        pltpu.VMEM((2, 256, HEADS * DH), BF16),
        pltpu.VMEM((2, 256, HEADS * DH), BF16),
        pltpu.SMEM((2,), jnp.int32),
        pltpu.VMEM((HEADS * DH,), F32),
        pltpu.VMEM((HEADS, 4, 4, 4, 16, DH), BF16),
        pltpu.VMEM((HEADS, 4, 272, DH), BF16),
        pltpu.VMEM((HEADS, 3, 272, DH), BF16),
        pltpu.VMEM((HEADS, 4, 80, DH), BF16),
        pltpu.VMEM((HEADS, 3, 80, DH), BF16),
        pltpu.VMEM((HEADS, 4, 32, DH), BF16),
        pltpu.VMEM((HEADS, 3, 32, DH), BF16),
        pltpu.VMEM((HEADS, 16, DH), F32),
        pltpu.VMEM((16, DH), F32),
        pltpu.VMEM((3, 16, DH), F32),
        pltpu.VMEM((HEADS, 2, DH, 256), BF16),
        pltpu.VMEM((2, 16, HEADS * DH), BF16),
        pltpu.VMEM((HEADS, 2, DH, DH), BF16),
        pltpu.VMEM((2, 272, DH), F32),
        dma((7,)),
        dma((3, 3, 3)), dma((3, 3, 3)), dma((3, 3, 3)), dma((3, 3, 3)), dma((3, 2, 3)), dma((3, 2, 3)),
        dma((HEADS, 3)), dma((HEADS, 3)), dma((HEADS, 3)), dma((HEADS, 3)),
        dma((HEADS, 3)), dma((HEADS, 3)), dma((HEADS, 3)), dma((HEADS, 3)),
        dma((3,)), dma((3,)),
    ]
    return pl.pallas_call(
        kernel,
        out_shape=jax.ShapeDtypeStruct(q_dec.shape, BF16),
        in_specs=[hbm] * 7,
        out_specs=pl.BlockSpec(memory_space=pltpu.VMEM),
        scratch_shapes=scratch,
        compiler_params=pltpu.CompilerParams(
            collective_id=0, has_side_effects=True, vmem_limit_bytes=62 << 20
        ),
        cost_estimate=pl.CostEstimate(flops=1_400_000_000, bytes_accessed=8_000_000, transcendentals=2_700_000),
        name="block_attention",
    )(q_dec, k_dec, v_dec, ctx_k, ctx_v, lengths, gain)


def solution(mesh):
    return jax.shard_map(
        per_device,
        mesh=mesh,
        in_specs=(
            P(None, "ctx", "tp"),
            P(None, "ctx", "tp"),
            P(None, "ctx", "tp"),
            P(None, "ctx", "tp"),
            P(None, "ctx", "tp"),
            P(),
            P("tp"),
        ),
        out_specs=P(None, "ctx", "tp"),
        check_vma=False,
    )
```

```python
import functools
import math

import jax
import jax.numpy as jnp
from jax import lax
from jax.experimental import pallas as pl
from jax.experimental.pallas import tpu as pltpu
from jax.sharding import PartitionSpec as P

MESH = pl.DeviceIdType.MESH
DH = 128
HEADS = 10
CHUNKS = ((0, 4), (4, 4), (8, 2))
ORDER = (("z", "y", "x"), ("z", "x", "y"), ("x", "y", "z"))
STRIDE = {"z": 16, "y": 4, "x": 1}
F32 = jnp.float32
BF16 = jnp.bfloat16
NT = (((1,), (1,)), ((), ()))
OFFS = (1, 3, 2)
STEPS, LAG1 = 5, 4
ATTEND = (0, 4, 3, 2, 1)


def kernel(
    q_hbm, kd_hbm, vd_hbm, ck_hbm, cv_hbm, len_hbm, gain_hbm, out_ref,
    q_ref, kd_ref, vd_ref, kbuf, vbuf, len_ref, gain_ref,
    qbuf, s1, r1, s2, r2, s3, r3, attended, nsend, nrecv, vt, kdp, vdt, bias,
    insem, g0s, g0r, g1s, g1r, g2s, g2r, g3s, g3r, r1s, r1r, r2s, r2r, r3s, r3r, ns, nr,
):
    ctx = lax.axis_index("ctx")
    tp = lax.axis_index("tp")
    loads = [
        pltpu.make_async_copy(src, dst, insem.at[i])
        for i, (src, dst) in enumerate((
            (q_hbm, q_ref), (kd_hbm, kd_ref), (vd_hbm, vd_ref), (ck_hbm, kbuf), (cv_hbm, vbuf), (len_hbm, len_ref), (gain_hbm, gain_ref),
        ))
    ]
    def along(stride, off):
        here = (ctx // stride) % 4
        return (ctx + ((here + off) % 4 - here) * stride, tp)

    barrier = pltpu.get_barrier_semaphore()
    for off in (1, 2, 3):
        for name in "zyx":
            pl.semaphore_signal(barrier, inc=1, device_id=along(STRIDE[name], off), device_id_type=MESH)
        pl.semaphore_signal(barrier, inc=1, device_id=(ctx, (tp + off) % 4), device_id_type=MESH)

    for load in loads:
        load.start()

    loads[0].wait()
    own = q_ref[...].astype(F32).reshape(16, HEADS * DH).astype(BF16)
    for h in range(HEADS):
        qbuf[h, 0, 0, 0] = own[:, h * DH : (h + 1) * DH]

    pl.semaphore_wait(barrier, 12)

    def remote(src, dst, send, recv, target):
        return pltpu.make_async_remote_copy(
            src_ref=src, dst_ref=dst, send_sem=send, recv_sem=recv, device_id=target, device_id_type=MESH
        )

    def heads(k):
        return pl.ds(CHUNKS[k][0], CHUNKS[k][1])

    def own_block(k, axis, off):
        spot = [0, 0, 0]
        spot[2 - axis] = off
        return remote(
            qbuf.at[heads(k), 0, 0, 0], qbuf.at[heads(k), spot[0], spot[1], spot[2]],
            g0s.at[k, axis, off - 1], g0r.at[k, axis, off - 1], along(STRIDE[ORDER[k][axis]], off),
        )

    def a_to_b(k, hop, off):
        return remote(
            qbuf.at[heads(k), 0, 0, hop], qbuf.at[heads(k), 0, off, hop],
            g1s.at[k, hop - 1, off - 1], g1r.at[k, hop - 1, off - 1], along(STRIDE[ORDER[k][1]], off),
        )

    def a_to_c(k, off):
        return remote(
            qbuf.at[heads(k), 0, 0, pl.ds(1, 3)], qbuf.at[heads(k), off, 0, pl.ds(1, 3)],
            g2s.at[k, 0, off - 1], g2r.at[k, 0, off - 1], along(STRIDE[ORDER[k][2]], off),
        )

    def b_to_c(k, off):
        return remote(
            qbuf.at[heads(k), 0, pl.ds(1, 3), 0], qbuf.at[heads(k), off, pl.ds(1, 3), 0],
            g2s.at[k, 1, off - 1], g2r.at[k, 1, off - 1], along(STRIDE[ORDER[k][2]], off),
        )

    def ab_to_c(h, k, off):
        return remote(
            qbuf.at[h, 0, pl.ds(1, 3), pl.ds(1, 3)], qbuf.at[h, off, pl.ds(1, 3), pl.ds(1, 3)],
            g3s.at[h, off - 1], g3r.at[h, off - 1], along(stride_c(k), off),
        )

    def pair(n):
        z = n // 4
        return ((8 * z + (1 - z) * n, 2 * z), (9 * z + (1 - z) * (4 + n), 1 + z))

    def stride_a(k):
        return 16 - 15 * (k * (k - 1) // 2)

    def stride_b(k):
        return 4 - 3 * (k * (2 - k))

    def stride_c(k):
        return 1 + 3 * k + 9 * (k * (k - 1) // 2)

    for k in (2, 0, 1):
        for off in OFFS:
            own_block(k, 0, off).start()
    for axis in (1, 2):
        for k in (2, 0, 1):
            for off in OFFS:
                own_block(k, axis, off).start()

    for load in loads[1:]:
        load.wait()
    row = lax.broadcasted_iota(jnp.int32, (256, DH), 0)
    dec_row = lax.broadcasted_iota(jnp.int32, (16, DH), 0)
    for s in range(2):
        limit = len_ref[s] - ctx * 256
        bias[s, 0:256] = jnp.where(row < limit, 0.0, -jnp.inf).astype(F32)
        bias[s, 256:272] = jnp.where(dec_row < 8, 0.0, -jnp.inf).astype(F32)
        pad = jnp.zeros((8, HEADS * DH), F32)
        kdp[s] = jnp.concatenate([kd_ref[s].astype(F32), pad], axis=0).astype(BF16)
        vpad = jnp.concatenate([vd_ref[s].astype(F32), jnp.zeros((DH - 8, HEADS * DH), F32)], axis=0)
        for h in range(HEADS):
            vdt[h, s] = vpad[:, h * DH : (h + 1) * DH].T.astype(BF16)

    for hop in OFFS:
        for k in (2, 0, 1):
            own_block(k, 0, hop).wait_recv()
            for off in OFFS:
                a_to_b(k, hop, off).start()
    for k in (2, 0, 1):
        for off in OFFS:
            a_to_c(k, off).start()
        for off in OFFS:
            own_block(k, 1, off).wait_recv()
        for off in OFFS:
            b_to_c(k, off).start()
    for k in (2, 0, 1):
        for hop in OFFS:
            for off in OFFS:
                a_to_b(k, hop, off).wait_recv()
    for n in ATTEND:
        for h, k in pair(n):
            for off in OFFS:
                ab_to_c(h, k, off).start()

    @pl.loop(0, HEADS)
    def _(h):
        lanes = pl.ds(pl.multiple_of(h * DH, DH), DH)
        for s in range(2):
            vt[h, s] = vbuf[s, :, lanes].astype(F32).T.astype(BF16)

    def first_back(h, k, off):
        return remote(s1.at[h, off], r1.at[h, off - 1], r1s.at[h, off - 1], r1r.at[h, off - 1], along(stride_c(k), 4 - off))

    def second_back(h, k, off):
        return remote(s2.at[h, off], r2.at[h, off - 1], r2s.at[h, off - 1], r2r.at[h, off - 1], along(stride_b(k), 4 - off))

    def third_back(h, k, off):
        return remote(s3.at[h, off], r3.at[h, off - 1], r3s.at[h, off - 1], r3r.at[h, off - 1], along(stride_a(k), 4 - off))

    scale = math.log2(math.e) / math.sqrt(DH)

    def split(lse):
        high = lse.astype(BF16).astype(F32)
        middle = (lse - high).astype(BF16).astype(F32)
        low = lse - high - middle
        return jnp.concatenate([high, middle, low, jnp.zeros((10, DH), F32)], axis=0).astype(BF16)

    def join(block):
        rows = block.astype(F32)
        return rows[0:2] + rows[2:4] + rows[4:6]

    def attend(h, offs):
        lanes = pl.ds(pl.multiple_of(h * DH, DH), DH)
        rows = [qbuf[h, off].reshape(16, 16, DH).astype(F32) for off in offs]
        lse = []
        for s in range(2):
            q = jnp.concatenate([x[:, 8 * s : 8 * s + 8, :].reshape(DH, DH) for x in rows], axis=0).astype(BF16)
            edge = jnp.concatenate([bias[s]] * len(offs), axis=1)
            x0 = lax.dot_general(kbuf[s, :, lanes], q, NT, preferred_element_type=F32) * scale + edge[0:256]
            x1 = lax.dot_general(kdp[s, :, lanes], q, NT, preferred_element_type=F32) * scale + edge[256:272]
            peak = jnp.maximum(jnp.max(x0, axis=0, keepdims=True), jnp.max(x1, axis=0, keepdims=True))
            w0 = jnp.exp2(x0 - peak)
            w1 = jnp.exp2(x1 - peak)
            total = jnp.sum(w0, axis=0, keepdims=True) + jnp.sum(w1, axis=0, keepdims=True)
            numer = jnp.dot(vt[h, s], w0.astype(BF16), preferred_element_type=F32)
            numer += jnp.dot(vdt[h, s, :, 0:16], w1.astype(BF16), preferred_element_type=F32)
            part = (numer * (1.0 / total)).astype(BF16)
            lse.append(peak + jnp.log2(total))
            for i, off in enumerate(offs):
                s1[h, off, DH * s : DH * s + DH] = part[:, DH * i : DH * i + DH]
        for i, off in enumerate(offs):
            s1[h, off, 256:272] = split(jnp.concatenate([x[:, DH * i : DH * i + DH] for x in lse], axis=0))

    def merge(parts):
        peak = functools.reduce(jnp.maximum, parts)
        weights = [jnp.exp2(part - peak) for part in parts]
        total = functools.reduce(jnp.add, weights)
        inverse = 1.0 / total
        return [w * inverse for w in weights], peak + jnp.log2(total)

    def shifted(rows, lanes):
        return pltpu.roll(rows, DH - lanes, 1) if lanes else rows

    def turned(factors):
        return jnp.concatenate(factors + [jnp.zeros((DH - 8, DH), F32)], axis=0).T

    def merge_first(t):
        for h, k in pair(t):
            for off in OFFS:
                first_back(h, k, off).wait_recv()
        results = []
        for h, k in pair(t):
            parts = [s1.at[h, 0]] + [r1.at[h, off - 1] for off in (1, 2, 3)]
            factors, lse = merge([join(part[256:272]) for part in parts])
            rows = []
            for s in range(2):
                acc = parts[0][DH * s : DH * s + DH].astype(F32) * factors[0][s : s + 1]
                for i in (1, 2, 3):
                    acc += parts[i][DH * s : DH * s + DH].astype(F32) * factors[i][s : s + 1]
                rows.append(acc.T.astype(BF16))
            results.append((h, rows, split(lse)))
        for h, rows, tail in results:
            for i in range(4):
                for s in range(2):
                    s2[h, i, 32 * s : 32 * s + 32] = rows[s][32 * i : 32 * i + 32]
                s2[h, i, 64:80] = tail
        for h, k in pair(t):
            for off in OFFS:
                second_back(h, k, off).start()

    def merge_second(t):
        for h, k in pair(t):
            for off in OFFS:
                second_back(h, k, off).wait_recv()
        results = []
        for h, k in pair(t):
            parts = [s2.at[h, 0]] + [r2.at[h, off - 1] for off in (1, 2, 3)]
            factors, lse = merge([shifted(join(part[64:80]), 32 * i) for i, part in enumerate(parts)])
            columns = turned(factors)[0:32]
            merged = []
            for s in range(2):
                acc = parts[0][32 * s : 32 * s + 32].astype(F32) * columns[:, s : s + 1]
                for i in (1, 2, 3):
                    acc += parts[i][32 * s : 32 * s + 32].astype(F32) * columns[:, 2 * i + s : 2 * i + s + 1]
                merged.append(acc)
            results.append((h, merged, split(lse)))
        for h, merged, tail in results:
            for i in range(4):
                s3[h, i, 0:16] = jnp.concatenate([m[8 * i : 8 * i + 8] for m in merged], axis=0).astype(BF16)
                s3[h, i, 16:32] = tail
        for h, k in pair(t):
            for off in OFFS:
                third_back(h, k, off).start()

    def merge_third(t):
        for h, k in pair(t):
            for off in OFFS:
                third_back(h, k, off).wait_recv()
        results = []
        for h, k in pair(t):
            parts = [s3.at[h, 0]] + [r3.at[h, off - 1] for off in (1, 2, 3)]
            factors, _ = merge([shifted(join(part[16:32]), 8 * i) for i, part in enumerate(parts)])
            columns = turned(factors)[0:8]
            acc = jnp.zeros((16, DH), F32)
            for i in range(4):
                column = jnp.concatenate([columns[:, 2 * i + s : 2 * i + s + 1] for s in range(2)], axis=0)
                acc += parts[i][0:16].astype(F32) * column
            results.append((h, acc))
        for h, acc in results:
            attended[h] = acc

    @pl.loop(0, STEPS)
    def _(t):
        for h, _ in pair(t):
            attend(h, (0,))

    for k in (2, 0, 1):
        for off in OFFS:
            own_block(k, 2, off).wait_recv()
            a_to_c(k, off).wait_recv()
            b_to_c(k, off).wait_recv()

    def merged(i):
        return ((i + 3) // 4) * (4 - i) + 4 * (i // 4)

    @pl.loop(0, STEPS)
    def _(t):
        for h, k in pair((4 * t) % 5):
            for off in OFFS:
                ab_to_c(h, k, off).wait_recv()
        for h, k in pair((4 * t) % 5):
            attend(h, (1, 3, 2))
            for off in OFFS:
                first_back(h, k, off).start()

        @pl.when(t >= LAG1)
        def _():
            merge_first(merged(t - LAG1))

    merge_first(merged(STEPS - LAG1))

    @pl.loop(0, STEPS - LAG1)
    def _(i):
        merge_second(merged(i))

    @pl.loop(STEPS - LAG1 + 1, STEPS)
    def _(i):
        merge_first(merged(i))

    @pl.loop(STEPS - LAG1, STEPS)
    def _(i):
        merge_second(merged(i))

    @pl.loop(0, STEPS)
    def _(i):
        merge_third(merged(i))

    squares = attended[0] * attended[0]
    for h in range(1, HEADS):
        squares += attended[h] * attended[h]
    nsend[...] = squares

    def norm(off):
        return remote(nsend, nrecv.at[off - 1], ns.at[off - 1], nr.at[off - 1], (ctx, (tp + off) % 4))

    for off in (1, 2, 3):
        norm(off).start()

    for k in range(3):
        for off in OFFS:
            for axis in range(3):
                own_block(k, axis, off).wait_send()
            for hop in OFFS:
                a_to_b(k, hop, off).wait_send()
            a_to_c(k, off).wait_send()
            b_to_c(k, off).wait_send()

    @pl.loop(0, STEPS)
    def _(t):
        for h, k in pair(t):
            for off in OFFS:
                ab_to_c(h, k, off).wait_send()
                first_back(h, k, off).wait_send()
                second_back(h, k, off).wait_send()
                third_back(h, k, off).wait_send()

    for off in (1, 2, 3):
        norm(off).wait()
    squares = squares + nrecv[0] + nrecv[1] + nrecv[2]
    mean = jnp.sum(squares, axis=1, keepdims=True) * (1.0 / (4 * HEADS * DH))
    inverse = lax.rsqrt(mean + 1e-06)
    for h in range(HEADS):
        y = attended[h] * inverse * gain_ref[h * DH : (h + 1) * DH].reshape(1, DH)
        for s in range(2):
            out_ref[s, :, h * DH : (h + 1) * DH] = y[8 * s : 8 * s + 8].astype(BF16)


def per_device(q_dec, k_dec, v_dec, ctx_k, ctx_v, lengths, gain):
    dma = pltpu.SemaphoreType.DMA
    hbm = pl.BlockSpec(memory_space=pltpu.HBM)
    scratch = [
        pltpu.VMEM((2, 8, HEADS * DH), BF16),
        pltpu.VMEM((2, 8, HEADS * DH), BF16),
        pltpu.VMEM((2, 8, HEADS * DH), BF16),
        pltpu.VMEM((2, 256, HEADS * DH), BF16),
        pltpu.VMEM((2, 256, HEADS * DH), BF16),
        pltpu.SMEM((2,), jnp.int32),
        pltpu.VMEM((HEADS * DH,), F32),
        pltpu.VMEM((HEADS, 4, 4, 4, 16, DH), BF16),
        pltpu.VMEM((HEADS, 4, 272, DH), BF16),
        pltpu.VMEM((HEADS, 3, 272, DH), BF16),
        pltpu.VMEM((HEADS, 4, 80, DH), BF16),
        pltpu.VMEM((HEADS, 3, 80, DH), BF16),
        pltpu.VMEM((HEADS, 4, 32, DH), BF16),
        pltpu.VMEM((HEADS, 3, 32, DH), BF16),
        pltpu.VMEM((HEADS, 16, DH), F32),
        pltpu.VMEM((16, DH), F32),
        pltpu.VMEM((3, 16, DH), F32),
        pltpu.VMEM((HEADS, 2, DH, 256), BF16),
        pltpu.VMEM((2, 16, HEADS * DH), BF16),
        pltpu.VMEM((HEADS, 2, DH, DH), BF16),
        pltpu.VMEM((2, 272, DH), F32),
        dma((7,)),
        dma((3, 3, 3)), dma((3, 3, 3)), dma((3, 3, 3)), dma((3, 3, 3)), dma((3, 2, 3)), dma((3, 2, 3)),
        dma((HEADS, 3)), dma((HEADS, 3)), dma((HEADS, 3)), dma((HEADS, 3)),
        dma((HEADS, 3)), dma((HEADS, 3)), dma((HEADS, 3)), dma((HEADS, 3)),
        dma((3,)), dma((3,)),
    ]
    return pl.pallas_call(
        kernel,
        out_shape=jax.ShapeDtypeStruct(q_dec.shape, BF16),
        in_specs=[hbm] * 7,
        out_specs=pl.BlockSpec(memory_space=pltpu.VMEM),
        scratch_shapes=scratch,
        compiler_params=pltpu.CompilerParams(
            collective_id=0, has_side_effects=True, vmem_limit_bytes=62 << 20
        ),
        cost_estimate=pl.CostEstimate(flops=1_400_000_000, bytes_accessed=8_000_000, transcendentals=2_700_000),
        name="block_attention",
    )(q_dec, k_dec, v_dec, ctx_k, ctx_v, lengths, gain)


def solution(mesh):
    return jax.shard_map(
        per_device,
        mesh=mesh,
        in_specs=(
            P(None, "ctx", "tp"),
            P(None, "ctx", "tp"),
            P(None, "ctx", "tp"),
            P(None, "ctx", "tp"),
            P(None, "ctx", "tp"),
            P(),
            P("tp"),
        ),
        out_specs=P(None, "ctx", "tp"),
        check_vma=False,
    )
```

```python
import functools
import math

import jax
import jax.numpy as jnp
from jax import lax
from jax.experimental import pallas as pl
from jax.experimental.pallas import tpu as pltpu
from jax.sharding import PartitionSpec as P

MESH = pl.DeviceIdType.MESH
DH = 128
HEADS = 10
CHUNKS = ((0, 4), (4, 4), (8, 2))
ORDER = (("z", "y", "x"), ("z", "x", "y"), ("x", "y", "z"))
STRIDE = {"z": 16, "y": 4, "x": 1}
F32 = jnp.float32
BF16 = jnp.bfloat16
NT = (((1,), (1,)), ((), ()))
OFFS = (1, 3, 2)
FAR = (2, 1, 3)
STEPS = 5
ATTEND = (0, 4, 3, 2, 1)


def kernel(
    q_hbm, kd_hbm, vd_hbm, ck_hbm, cv_hbm, len_hbm, gain_hbm, out_ref,
    q_ref, kd_ref, vd_ref, kbuf, vbuf, len_ref, gain_ref,
    qbuf, s1, r1, s2, r2, s3, r3, attended, nsend, nrecv, vt, kdp, vdb, bias,
    insem, g0s, g0r, g1s, g1r, g2s, g2r, g3s, g3r, r1s, r1r, r2s, r2r, r3s, r3r, ns, nr,
):
    ctx = lax.axis_index("ctx")
    tp = lax.axis_index("tp")
    loads = [
        pltpu.make_async_copy(src, dst, insem.at[i])
        for i, (src, dst) in enumerate((
            (q_hbm, q_ref), (kd_hbm, kd_ref), (vd_hbm, vd_ref), (ck_hbm, kbuf), (cv_hbm, vbuf), (len_hbm, len_ref), (gain_hbm, gain_ref),
        ))
    ]
    def along(stride, off):
        here = (ctx // stride) % 4
        return (ctx + ((here + off) % 4 - here) * stride, tp)

    barrier = pltpu.get_barrier_semaphore()
    for off in (2, 1, 3):
        for name in "zyx":
            pl.semaphore_signal(barrier, inc=1, device_id=along(STRIDE[name], off), device_id_type=MESH)
        pl.semaphore_signal(barrier, inc=1, device_id=(ctx, (tp + off) % 4), device_id_type=MESH)

    for load in loads:
        load.start()

    loads[0].wait()
    own = q_ref[...].astype(F32).reshape(16, HEADS * DH).astype(BF16)
    for h in range(HEADS):
        qbuf[h, 0, 0, 0] = own[:, h * DH : (h + 1) * DH]

    pl.semaphore_wait(barrier, 12)

    def remote(src, dst, send, recv, target):
        return pltpu.make_async_remote_copy(
            src_ref=src, dst_ref=dst, send_sem=send, recv_sem=recv, device_id=target, device_id_type=MESH
        )

    def heads(k):
        return pl.ds(CHUNKS[k][0], CHUNKS[k][1])

    def own_z(off):
        both = pl.ds(0, 8)
        return remote(
            qbuf.at[both, 0, 0, 0], qbuf.at[both, 0, 0, off],
            g0s.at[0, 0, off - 1], g0r.at[0, 0, off - 1], along(STRIDE["z"], off),
        )

    def own_block(k, axis, off):
        spot = [0, 0, 0]
        spot[2 - axis] = off
        return remote(
            qbuf.at[heads(k), 0, 0, 0], qbuf.at[heads(k), spot[0], spot[1], spot[2]],
            g0s.at[k, axis, off - 1], g0r.at[k, axis, off - 1], along(STRIDE[ORDER[k][axis]], off),
        )

    def a_to_b(k, hop, off):
        return remote(
            qbuf.at[heads(k), 0, 0, hop], qbuf.at[heads(k), 0, off, hop],
            g1s.at[k, hop - 1, off - 1], g1r.at[k, hop - 1, off - 1], along(STRIDE[ORDER[k][1]], off),
        )

    def a_to_c(k, off):
        return remote(
            qbuf.at[heads(k), 0, 0, pl.ds(1, 3)], qbuf.at[heads(k), off, 0, pl.ds(1, 3)],
            g2s.at[k, 0, off - 1], g2r.at[k, 0, off - 1], along(STRIDE[ORDER[k][2]], off),
        )

    def b_to_c(k, off):
        return remote(
            qbuf.at[heads(k), 0, pl.ds(1, 3), 0], qbuf.at[heads(k), off, pl.ds(1, 3), 0],
            g2s.at[k, 1, off - 1], g2r.at[k, 1, off - 1], along(STRIDE[ORDER[k][2]], off),
        )

    def ab_to_c(h, k, off):
        return remote(
            qbuf.at[h, 0, pl.ds(1, 3), pl.ds(1, 3)], qbuf.at[h, off, pl.ds(1, 3), pl.ds(1, 3)],
            g3s.at[h, off - 1], g3r.at[h, off - 1], along(stride_c(k), off),
        )

    def pair(n):
        z = n // 4
        return ((8 * z + (1 - z) * n, 2 * z), (9 * z + (1 - z) * (4 + n), 1 + z))

    def stride_a(k):
        return 16 - 15 * (k * (k - 1) // 2)

    def stride_b(k):
        return 4 - 3 * (k * (2 - k))

    def stride_c(k):
        return 1 + 3 * k + 9 * (k * (k - 1) // 2)

    for off in FAR:
        own_z(off).start()
    for off in FAR:
        own_block(2, 0, off).start()
    for axis in (1, 2):
        for k in (2, 0, 1):
            for off in FAR:
                own_block(k, axis, off).start()

    for load in loads[1:]:
        load.wait()
    row = lax.broadcasted_iota(jnp.int32, (256, DH), 0)
    dec_row = lax.broadcasted_iota(jnp.int32, (16, DH), 0)
    for s in range(2):
        limit = len_ref[s] - ctx * 256
        bias[s, 0:256] = jnp.where(row < limit, 0.0, -jnp.inf).astype(F32)
        bias[s, 256:272] = jnp.where(dec_row < 8, 0.0, -jnp.inf).astype(F32)
        pad = jnp.zeros((8, HEADS * DH), F32)
        kdp[s] = jnp.concatenate([kd_ref[s].astype(F32), pad], axis=0).astype(BF16)
        vpad = jnp.concatenate([vd_ref[s].astype(F32), jnp.zeros((DH - 8, HEADS * DH), F32)], axis=0)
        for h in range(HEADS):
            turned_values = vpad[:, h * DH : (h + 1) * DH].T
            for j in range(8):
                vdb[h, s, j] = jnp.broadcast_to(turned_values[:, j : j + 1], (DH, DH))

    for hop in OFFS:
        for k in (2, 0, 1):
            if k == 0:
                own_z(hop).wait_recv()
            if k == 2:
                own_block(k, 0, hop).wait_recv()
            for off in FAR:
                a_to_b(k, hop, off).start()
    for k in (2, 0, 1):
        for off in FAR:
            a_to_c(k, off).start()
        for off in OFFS:
            own_block(k, 1, off).wait_recv()
        for off in FAR:
            b_to_c(k, off).start()
    for k in (2, 0, 1):
        for hop in OFFS:
            for off in OFFS:
                a_to_b(k, hop, off).wait_recv()
    for n in ATTEND:
        for h, k in pair(n):
            for off in FAR:
                ab_to_c(h, k, off).start()

    @pl.loop(0, HEADS)
    def _(h):
        lanes = pl.ds(pl.multiple_of(h * DH, DH), DH)
        for s in range(2):
            vt[h, s] = vbuf[s, :, lanes].astype(F32).T.astype(BF16)

    def first_back(h, k, off):
        return remote(s1.at[h, off], r1.at[h, off - 1], r1s.at[h, off - 1], r1r.at[h, off - 1], along(stride_c(k), 4 - off))

    def second_back(h, k, off):
        return remote(s2.at[h, off], r2.at[h, off - 1], r2s.at[h, off - 1], r2r.at[h, off - 1], along(stride_b(k), 4 - off))

    def third_back(h, k, off):
        return remote(s3.at[h, off], r3.at[h, off - 1], r3s.at[h, off - 1], r3r.at[h, off - 1], along(stride_a(k), 4 - off))

    scale = math.log2(math.e) / math.sqrt(DH)

    def split(lse):
        high = lse.astype(BF16).astype(F32)
        middle = (lse - high).astype(BF16).astype(F32)
        low = lse - high - middle
        return jnp.concatenate([high, middle, low, jnp.zeros((10, DH), F32)], axis=0).astype(BF16)

    def join(block):
        rows = block.astype(F32)
        return rows[0:2] + rows[2:4] + rows[4:6]

    def attend(h, offs):
        lanes = pl.ds(pl.multiple_of(h * DH, DH), DH)
        rows = [qbuf[h, off].reshape(16, 16, DH).astype(F32) for off in offs]
        lse = []
        for s in range(2):
            q = jnp.concatenate([x[:, 8 * s : 8 * s + 8, :].reshape(DH, DH) for x in rows], axis=0).astype(BF16)
            edge = jnp.concatenate([bias[s]] * len(offs), axis=1)
            x0 = lax.dot_general(kbuf[s, :, lanes], q, NT, preferred_element_type=F32) * scale + edge[0:256]
            x1 = lax.dot_general(kdp[s, :, lanes], q, NT, preferred_element_type=F32) * scale + edge[256:272]
            peak = jnp.maximum(jnp.max(x0, axis=0, keepdims=True), jnp.max(x1, axis=0, keepdims=True))
            w0 = jnp.exp2(x0 - peak)
            w1 = jnp.exp2(x1 - peak)
            total = jnp.sum(w0, axis=0, keepdims=True) + jnp.sum(w1, axis=0, keepdims=True)
            numer = jnp.dot(vt[h, s], w0.astype(BF16), preferred_element_type=F32)
            w1 = w1.astype(BF16).astype(F32)
            block = []
            for i in range(len(offs)):
                own_part = vdb[h, s, 0] * w1[0:1, DH * i : DH * i + DH]
                for j in range(1, 8):
                    own_part += vdb[h, s, j] * w1[j : j + 1, DH * i : DH * i + DH]
                block.append(own_part)
            numer += jnp.concatenate(block, axis=1)
            part = (numer * (1.0 / total)).astype(BF16)
            lse.append(peak + jnp.log2(total))
            for i, off in enumerate(offs):
                s1[h, off, DH * s : DH * s + DH] = part[:, DH * i : DH * i + DH]
        for i, off in enumerate(offs):
            s1[h, off, 256:272] = split(jnp.concatenate([x[:, DH * i : DH * i + DH] for x in lse], axis=0))

    def merge(parts):
        peak = functools.reduce(jnp.maximum, parts)
        weights = [jnp.exp2(part - peak) for part in parts]
        total = functools.reduce(jnp.add, weights)
        inverse = 1.0 / total
        return [w * inverse for w in weights], peak + jnp.log2(total)

    def shifted(rows, lanes):
        return pltpu.roll(rows, DH - lanes, 1) if lanes else rows

    def turned(factors):
        return jnp.concatenate(factors + [jnp.zeros((DH - 8, DH), F32)], axis=0).T

    def merge_first(*pairs):
        todo = [entry for n in pairs for entry in pair(n)]
        for h, k in todo:
            for off in OFFS:
                first_back(h, k, off).wait_recv()
        results = []
        for h, k in todo:
            parts = [s1.at[h, 0]] + [r1.at[h, off - 1] for off in (1, 2, 3)]
            factors, lse = merge([join(part[256:272]) for part in parts])
            rows = []
            for s in range(2):
                acc = parts[0][DH * s : DH * s + DH].astype(F32) * factors[0][s : s + 1]
                for i in (1, 2, 3):
                    acc += parts[i][DH * s : DH * s + DH].astype(F32) * factors[i][s : s + 1]
                rows.append(acc.T.astype(BF16))
            results.append((h, rows, split(lse)))
        for h, rows, tail in results:
            for i in range(4):
                for s in range(2):
                    s2[h, i, 32 * s : 32 * s + 32] = rows[s][32 * i : 32 * i + 32]
                s2[h, i, 64:80] = tail
        for h, k in todo:
            for off in FAR:
                second_back(h, k, off).start()

    def merge_second(*pairs):
        todo = [entry for n in pairs for entry in pair(n)]
        for h, k in todo:
            for off in OFFS:
                second_back(h, k, off).wait_recv()
        results = []
        for h, k in todo:
            parts = [s2.at[h, 0]] + [r2.at[h, off - 1] for off in (1, 2, 3)]
            factors, lse = merge([shifted(join(part[64:80]), 32 * i) for i, part in enumerate(parts)])
            columns = turned(factors)[0:32]
            merged = []
            for s in range(2):
                acc = parts[0][32 * s : 32 * s + 32].astype(F32) * columns[:, s : s + 1]
                for i in (1, 2, 3):
                    acc += parts[i][32 * s : 32 * s + 32].astype(F32) * columns[:, 2 * i + s : 2 * i + s + 1]
                merged.append(acc)
            results.append((h, merged, split(lse)))
        for h, merged, tail in results:
            for i in range(4):
                s3[h, i, 0:16] = jnp.concatenate([m[8 * i : 8 * i + 8] for m in merged], axis=0).astype(BF16)
                s3[h, i, 16:32] = tail
        for h, k in todo:
            for off in FAR:
                third_back(h, k, off).start()

    def merge_third(*pairs):
        todo = [entry for n in pairs for entry in pair(n)]
        for h, k in todo:
            for off in OFFS:
                third_back(h, k, off).wait_recv()
        results = []
        for h, k in todo:
            parts = [s3.at[h, 0]] + [r3.at[h, off - 1] for off in (1, 2, 3)]
            factors, _ = merge([shifted(join(part[16:32]), 8 * i) for i, part in enumerate(parts)])
            columns = turned(factors)[0:8]
            acc = jnp.zeros((16, DH), F32)
            for i in range(4):
                column = jnp.concatenate([columns[:, 2 * i + s : 2 * i + s + 1] for s in range(2)], axis=0)
                acc += parts[i][0:16].astype(F32) * column
            results.append((h, acc))
        for h, acc in results:
            attended[h] = acc

    @pl.loop(0, STEPS)
    def _(t):
        for h, _ in pair(t):
            attend(h, (0,))

    for k in (2, 0, 1):
        for off in OFFS:
            own_block(k, 2, off).wait_recv()
            a_to_c(k, off).wait_recv()
            b_to_c(k, off).wait_recv()

    @pl.loop(0, STEPS)
    def _(t):
        for h, k in pair((4 * t) % 5):
            for off in OFFS:
                ab_to_c(h, k, off).wait_recv()
        for h, k in pair((4 * t) % 5):
            attend(h, (1, 3, 2))
            for off in FAR:
                first_back(h, k, off).start()

    merge_first(0, 3, 2)
    merge_first(1, 4)
    merge_second(0, 3, 2)
    merge_second(1, 4)
    merge_third(0, 3, 2, 1, 4)

    squares = attended[0] * attended[0]
    for h in range(1, HEADS):
        squares += attended[h] * attended[h]
    nsend[...] = squares

    def norm(off):
        return remote(nsend, nrecv.at[off - 1], ns.at[off - 1], nr.at[off - 1], (ctx, (tp + off) % 4))

    for off in (1, 2, 3):
        norm(off).start()

    for k in range(3):
        for off in OFFS:
            for axis in range(3):
                if axis > 0 or k == 2:
                    own_block(k, axis, off).wait_send()
            if k == 0:
                own_z(off).wait_send()
            for hop in OFFS:
                a_to_b(k, hop, off).wait_send()
            a_to_c(k, off).wait_send()
            b_to_c(k, off).wait_send()

    @pl.loop(0, STEPS)
    def _(t):
        for h, k in pair(t):
            for off in OFFS:
                ab_to_c(h, k, off).wait_send()
                first_back(h, k, off).wait_send()
                second_back(h, k, off).wait_send()
                third_back(h, k, off).wait_send()

    for off in (1, 2, 3):
        norm(off).wait()
    squares = squares + nrecv[0] + nrecv[1] + nrecv[2]
    mean = jnp.sum(squares, axis=1, keepdims=True) * (1.0 / (4 * HEADS * DH))
    inverse = lax.rsqrt(mean + 1e-06)
    for h in range(HEADS):
        y = attended[h] * inverse * gain_ref[h * DH : (h + 1) * DH].reshape(1, DH)
        for s in range(2):
            out_ref[s, :, h * DH : (h + 1) * DH] = y[8 * s : 8 * s + 8].astype(BF16)


def per_device(q_dec, k_dec, v_dec, ctx_k, ctx_v, lengths, gain):
    dma = pltpu.SemaphoreType.DMA
    hbm = pl.BlockSpec(memory_space=pltpu.HBM)
    scratch = [
        pltpu.VMEM((2, 8, HEADS * DH), BF16),
        pltpu.VMEM((2, 8, HEADS * DH), BF16),
        pltpu.VMEM((2, 8, HEADS * DH), BF16),
        pltpu.VMEM((2, 256, HEADS * DH), BF16),
        pltpu.VMEM((2, 256, HEADS * DH), BF16),
        pltpu.SMEM((2,), jnp.int32),
        pltpu.VMEM((HEADS * DH,), F32),
        pltpu.VMEM((HEADS, 4, 4, 4, 16, DH), BF16),
        pltpu.VMEM((HEADS, 4, 272, DH), BF16),
        pltpu.VMEM((HEADS, 3, 272, DH), BF16),
        pltpu.VMEM((HEADS, 4, 80, DH), BF16),
        pltpu.VMEM((HEADS, 3, 80, DH), BF16),
        pltpu.VMEM((HEADS, 4, 32, DH), BF16),
        pltpu.VMEM((HEADS, 3, 32, DH), BF16),
        pltpu.VMEM((HEADS, 16, DH), F32),
        pltpu.VMEM((16, DH), F32),
        pltpu.VMEM((3, 16, DH), F32),
        pltpu.VMEM((HEADS, 2, DH, 256), BF16),
        pltpu.VMEM((2, 16, HEADS * DH), BF16),
        pltpu.VMEM((HEADS, 2, 8, DH, DH), F32),
        pltpu.VMEM((2, 272, DH), F32),
        dma((7,)),
        dma((3, 3, 3)), dma((3, 3, 3)), dma((3, 3, 3)), dma((3, 3, 3)), dma((3, 2, 3)), dma((3, 2, 3)),
        dma((HEADS, 3)), dma((HEADS, 3)), dma((HEADS, 3)), dma((HEADS, 3)),
        dma((HEADS, 3)), dma((HEADS, 3)), dma((HEADS, 3)), dma((HEADS, 3)),
        dma((3,)), dma((3,)),
    ]
    return pl.pallas_call(
        kernel,
        out_shape=jax.ShapeDtypeStruct(q_dec.shape, BF16),
        in_specs=[hbm] * 7,
        out_specs=pl.BlockSpec(memory_space=pltpu.VMEM),
        scratch_shapes=scratch,
        compiler_params=pltpu.CompilerParams(
            collective_id=0, has_side_effects=True, vmem_limit_bytes=62 << 20
        ),
        cost_estimate=pl.CostEstimate(flops=1_400_000_000, bytes_accessed=8_000_000, transcendentals=2_700_000),
        name="block_attention",
    )(q_dec, k_dec, v_dec, ctx_k, ctx_v, lengths, gain)


def solution(mesh):
    return jax.shard_map(
        per_device,
        mesh=mesh,
        in_specs=(
            P(None, "ctx", "tp"),
            P(None, "ctx", "tp"),
            P(None, "ctx", "tp"),
            P(None, "ctx", "tp"),
            P(None, "ctx", "tp"),
            P(),
            P("tp"),
        ),
        out_specs=P(None, "ctx", "tp"),
        check_vma=False,
    )
```

```python
import functools
import math

import jax
import jax.numpy as jnp
from jax import lax
from jax.experimental import pallas as pl
from jax.experimental.pallas import tpu as pltpu
from jax.sharding import PartitionSpec as P

MESH = pl.DeviceIdType.MESH
DH = 128
HEADS = 10
CHUNKS = ((0, 4), (4, 4), (8, 2))
ORDER = (("z", "y", "x"), ("z", "x", "y"), ("x", "y", "z"))
STRIDE = {"z": 16, "y": 4, "x": 1}
F32 = jnp.float32
BF16 = jnp.bfloat16
NT = (((1,), (1,)), ((), ()))
OFFS = (1, 3, 2)
FAR = (2, 1, 3)
STEPS = 5
ATTEND = (0, 4, 3, 2, 1)


def kernel(
    q_hbm, kd_hbm, vd_hbm, ck_hbm, cv_hbm, len_hbm, gain_hbm, out_ref,
    q_ref, kd_ref, vd_ref, kbuf, vbuf, len_ref, gain_ref,
    qbuf, s1, r1, s2, r2, s3, r3, attended, nsend, nrecv, vt, kdp, vdb, bias,
    insem, g0s, g0r, g1s, g1r, g2s, g2r, g3s, g3r, r1s, r1r, r2s, r2r, r3s, r3r, ns, nr,
):
    ctx = lax.axis_index("ctx")
    tp = lax.axis_index("tp")
    loads = [
        pltpu.make_async_copy(src, dst, insem.at[i])
        for i, (src, dst) in enumerate((
            (q_hbm, q_ref), (kd_hbm, kd_ref), (vd_hbm, vd_ref), (ck_hbm, kbuf), (cv_hbm, vbuf), (len_hbm, len_ref), (gain_hbm, gain_ref),
        ))
    ]
    def along(stride, off):
        here = (ctx // stride) % 4
        return (ctx + ((here + off) % 4 - here) * stride, tp)

    barrier = pltpu.get_barrier_semaphore()
    for off in (2, 1, 3):
        for name in "zyx":
            pl.semaphore_signal(barrier, inc=1, device_id=along(STRIDE[name], off), device_id_type=MESH)
        pl.semaphore_signal(barrier, inc=1, device_id=(ctx, (tp + off) % 4), device_id_type=MESH)

    for load in loads:
        load.start()

    loads[0].wait()
    own = q_ref[...].astype(F32).reshape(16, HEADS * DH).astype(BF16)
    for h in range(HEADS):
        qbuf[h, 0, 0, 0] = own[:, h * DH : (h + 1) * DH]

    pl.semaphore_wait(barrier, 12)

    def remote(src, dst, send, recv, target):
        return pltpu.make_async_remote_copy(
            src_ref=src, dst_ref=dst, send_sem=send, recv_sem=recv, device_id=target, device_id_type=MESH
        )

    def heads(k):
        return pl.ds(CHUNKS[k][0], CHUNKS[k][1])

    def own_z(off):
        both = pl.ds(0, 8)
        return remote(
            qbuf.at[both, 0, 0, 0], qbuf.at[both, 0, 0, off],
            g0s.at[0, 0, off - 1], g0r.at[0, 0, off - 1], along(STRIDE["z"], off),
        )

    def own_block(k, axis, off):
        spot = [0, 0, 0]
        spot[2 - axis] = off
        return remote(
            qbuf.at[heads(k), 0, 0, 0], qbuf.at[heads(k), spot[0], spot[1], spot[2]],
            g0s.at[k, axis, off - 1], g0r.at[k, axis, off - 1], along(STRIDE[ORDER[k][axis]], off),
        )

    def a_to_b(k, hop, off):
        return remote(
            qbuf.at[heads(k), 0, 0, hop], qbuf.at[heads(k), 0, off, hop],
            g1s.at[k, hop - 1, off - 1], g1r.at[k, hop - 1, off - 1], along(STRIDE[ORDER[k][1]], off),
        )

    def a_to_c(k, off):
        return remote(
            qbuf.at[heads(k), 0, 0, pl.ds(1, 3)], qbuf.at[heads(k), off, 0, pl.ds(1, 3)],
            g2s.at[k, 0, off - 1], g2r.at[k, 0, off - 1], along(STRIDE[ORDER[k][2]], off),
        )

    def b_to_c(k, off):
        return remote(
            qbuf.at[heads(k), 0, pl.ds(1, 3), 0], qbuf.at[heads(k), off, pl.ds(1, 3), 0],
            g2s.at[k, 1, off - 1], g2r.at[k, 1, off - 1], along(STRIDE[ORDER[k][2]], off),
        )

    def ab_to_c(h, k, off):
        return remote(
            qbuf.at[h, 0, pl.ds(1, 3), pl.ds(1, 3)], qbuf.at[h, off, pl.ds(1, 3), pl.ds(1, 3)],
            g3s.at[h, off - 1], g3r.at[h, off - 1], along(stride_c(k), off),
        )

    def pair(n):
        z = n // 4
        return ((8 * z + (1 - z) * n, 2 * z), (9 * z + (1 - z) * (4 + n), 1 + z))

    def stride_a(k):
        return 16 - 15 * (k * (k - 1) // 2)

    def stride_b(k):
        return 4 - 3 * (k * (2 - k))

    def stride_c(k):
        return 1 + 3 * k + 9 * (k * (k - 1) // 2)

    for off in FAR:
        own_z(off).start()
    for off in FAR:
        own_block(2, 0, off).start()
    for axis in (1, 2):
        for k in (2, 0, 1):
            for off in FAR:
                own_block(k, axis, off).start()

    for load in loads[1:]:
        load.wait()
    row = lax.broadcasted_iota(jnp.int32, (256, DH), 0)
    dec_row = lax.broadcasted_iota(jnp.int32, (16, DH), 0)
    for s in range(2):
        limit = len_ref[s] - ctx * 256
        bias[s, 0:256] = jnp.where(row < limit, 0.0, -jnp.inf).astype(F32)
        bias[s, 256:272] = jnp.where(dec_row < 8, 0.0, -jnp.inf).astype(F32)
        pad = jnp.zeros((8, HEADS * DH), F32)
        kdp[s] = jnp.concatenate([kd_ref[s].astype(F32), pad], axis=0).astype(BF16)
        vpad = jnp.concatenate([vd_ref[s].astype(F32), jnp.zeros((DH - 8, HEADS * DH), F32)], axis=0)
        for h in range(HEADS):
            turned_values = vpad[:, h * DH : (h + 1) * DH].T
            for j in range(8):
                vdb[h, s, j] = jnp.broadcast_to(turned_values[:, j : j + 1], (DH, DH))

    for hop in OFFS:
        for k in (2, 0, 1):
            if k == 0:
                own_z(hop).wait_recv()
            if k == 2:
                own_block(k, 0, hop).wait_recv()
            for off in FAR:
                a_to_b(k, hop, off).start()
    for k in (2, 0, 1):
        for off in FAR:
            a_to_c(k, off).start()
        for off in OFFS:
            own_block(k, 1, off).wait_recv()
        for off in FAR:
            b_to_c(k, off).start()
    for k in (2, 0, 1):
        for hop in OFFS:
            for off in OFFS:
                a_to_b(k, hop, off).wait_recv()
    for n in ATTEND:
        for h, k in pair(n):
            for off in FAR:
                ab_to_c(h, k, off).start()

    @pl.loop(0, HEADS)
    def _(h):
        lanes = pl.ds(pl.multiple_of(h * DH, DH), DH)
        for s in range(2):
            vt[h, s] = vbuf[s, :, lanes].astype(F32).T.astype(BF16)

    def first_back(h, k, off):
        return remote(s1.at[h, off], r1.at[h, off - 1], r1s.at[h, off - 1], r1r.at[h, off - 1], along(stride_c(k), 4 - off))

    def second_back(h, k, off):
        return remote(s2.at[h, off], r2.at[h, off - 1], r2s.at[h, off - 1], r2r.at[h, off - 1], along(stride_b(k), 4 - off))

    def third_back(n, off):
        k = 2 * (n // 4)
        return remote(s3.at[n, off], r3.at[n, off - 1], r3s.at[n, off - 1], r3r.at[n, off - 1], along(stride_a(k), 4 - off))

    scale = math.log2(math.e) / math.sqrt(DH)

    def split(*lses):
        rows = []
        for lse in lses:
            high = lse.astype(BF16).astype(F32)
            middle = (lse - high).astype(BF16).astype(F32)
            rows += [high, middle, lse - high - middle]
        rows.append(jnp.zeros((16 - 6 * len(lses), DH), F32))
        return jnp.concatenate(rows, axis=0).astype(BF16)

    def join(block, i=0):
        rows = block.astype(F32)[6 * i : 6 * i + 6]
        return rows[0:2] + rows[2:4] + rows[4:6]

    def attend(h, offs):
        lanes = pl.ds(pl.multiple_of(h * DH, DH), DH)
        rows = [qbuf[h, off].reshape(16, 16, DH).astype(F32) for off in offs]
        lse = []
        for s in range(2):
            q = jnp.concatenate([x[:, 8 * s : 8 * s + 8, :].reshape(DH, DH) for x in rows], axis=0).astype(BF16)
            edge = jnp.concatenate([bias[s]] * len(offs), axis=1)
            x0 = lax.dot_general(kbuf[s, :, lanes], q, NT, preferred_element_type=F32) * scale + edge[0:256]
            x1 = lax.dot_general(kdp[s, :, lanes], q, NT, preferred_element_type=F32) * scale + edge[256:272]
            peak = jnp.maximum(jnp.max(x0, axis=0, keepdims=True), jnp.max(x1, axis=0, keepdims=True))
            w0 = jnp.exp2(x0 - peak)
            w1 = jnp.exp2(x1 - peak)
            total = jnp.sum(w0, axis=0, keepdims=True) + jnp.sum(w1, axis=0, keepdims=True)
            numer = jnp.dot(vt[h, s], w0.astype(BF16), preferred_element_type=F32)
            w1 = w1.astype(BF16).astype(F32)
            block = []
            for i in range(len(offs)):
                own_part = vdb[h, s, 0] * w1[0:1, DH * i : DH * i + DH]
                for j in range(1, 8):
                    own_part += vdb[h, s, j] * w1[j : j + 1, DH * i : DH * i + DH]
                block.append(own_part)
            numer += jnp.concatenate(block, axis=1)
            part = (numer * (1.0 / total)).astype(BF16)
            lse.append(peak + jnp.log2(total))
            for i, off in enumerate(offs):
                s1[h, off, DH * s : DH * s + DH] = part[:, DH * i : DH * i + DH]
        for i, off in enumerate(offs):
            s1[h, off, 256:272] = split(jnp.concatenate([x[:, DH * i : DH * i + DH] for x in lse], axis=0))

    def merge(parts):
        peak = functools.reduce(jnp.maximum, parts)
        weights = [jnp.exp2(part - peak) for part in parts]
        total = functools.reduce(jnp.add, weights)
        inverse = 1.0 / total
        return [w * inverse for w in weights], peak + jnp.log2(total)

    def shifted(rows, lanes):
        return pltpu.roll(rows, DH - lanes, 1) if lanes else rows

    def turned(factors):
        return jnp.concatenate(factors + [jnp.zeros((DH - 8, DH), F32)], axis=0).T

    def merge_first(*pairs):
        todo = [entry for n in pairs for entry in pair(n)]
        for h, k in todo:
            for off in OFFS:
                first_back(h, k, off).wait_recv()
        results = []
        for h, k in todo:
            parts = [s1.at[h, 0]] + [r1.at[h, off - 1] for off in (1, 2, 3)]
            factors, lse = merge([join(part[256:272]) for part in parts])
            rows = []
            for s in range(2):
                acc = parts[0][DH * s : DH * s + DH].astype(F32) * factors[0][s : s + 1]
                for i in (1, 2, 3):
                    acc += parts[i][DH * s : DH * s + DH].astype(F32) * factors[i][s : s + 1]
                rows.append(acc.T.astype(BF16))
            results.append((h, rows, split(lse)))
        for h, rows, tail in results:
            for i in range(4):
                for s in range(2):
                    s2[h, i, 32 * s : 32 * s + 32] = rows[s][32 * i : 32 * i + 32]
                s2[h, i, 64:80] = tail
        for h, k in todo:
            for off in FAR:
                second_back(h, k, off).start()

    def merge_second(*pairs):
        todo = [entry for n in pairs for entry in pair(n)]
        for h, k in todo:
            for off in OFFS:
                second_back(h, k, off).wait_recv()
        results = []
        for h, k in todo:
            parts = [s2.at[h, 0]] + [r2.at[h, off - 1] for off in (1, 2, 3)]
            factors, lse = merge([shifted(join(part[64:80]), 32 * i) for i, part in enumerate(parts)])
            columns = turned(factors)[0:32]
            merged = []
            for s in range(2):
                acc = parts[0][32 * s : 32 * s + 32].astype(F32) * columns[:, s : s + 1]
                for i in (1, 2, 3):
                    acc += parts[i][32 * s : 32 * s + 32].astype(F32) * columns[:, 2 * i + s : 2 * i + s + 1]
                merged.append(acc)
            results.append((merged, lse))
        for p, n in enumerate(pairs):
            tail = split(results[2 * p][1], results[2 * p + 1][1])
            for i in range(4):
                for e in range(2):
                    rows = [m[8 * i : 8 * i + 8] for m in results[2 * p + e][0]]
                    s3[n, i, 16 * e : 16 * e + 16] = jnp.concatenate(rows, axis=0).astype(BF16)
                s3[n, i, 32:48] = tail
        for n in pairs:
            for off in FAR:
                third_back(n, off).start()

    def merge_third(*pairs):
        for n in pairs:
            for off in OFFS:
                third_back(n, off).wait_recv()
        results = []
        for n in pairs:
            parts = [s3.at[n, 0]] + [r3.at[n, off - 1] for off in (1, 2, 3)]
            for e, (h, _) in enumerate(pair(n)):
                factors, _ = merge([shifted(join(part[32:48], e), 8 * i) for i, part in enumerate(parts)])
                columns = turned(factors)[0:8]
                acc = jnp.zeros((16, DH), F32)
                for i in range(4):
                    column = jnp.concatenate([columns[:, 2 * i + s : 2 * i + s + 1] for s in range(2)], axis=0)
                    acc += parts[i][16 * e : 16 * e + 16].astype(F32) * column
                results.append((h, acc))
        for h, acc in results:
            attended[h] = acc

    @pl.loop(0, STEPS)
    def _(t):
        for h, _ in pair(t):
            attend(h, (0,))

    for k in (2, 0, 1):
        for off in OFFS:
            own_block(k, 2, off).wait_recv()
            a_to_c(k, off).wait_recv()
            b_to_c(k, off).wait_recv()

    @pl.loop(0, STEPS)
    def _(t):
        for h, k in pair((4 * t) % 5):
            for off in OFFS:
                ab_to_c(h, k, off).wait_recv()
        for h, k in pair((4 * t) % 5):
            attend(h, (1, 3, 2))
            for off in FAR:
                first_back(h, k, off).start()

    merge_first(0, 3, 2)
    merge_first(1, 4)
    merge_second(0, 3, 2)
    merge_second(1, 4)
    merge_third(0, 3, 2, 1, 4)

    squares = attended[0] * attended[0]
    for h in range(1, HEADS):
        squares += attended[h] * attended[h]
    nsend[...] = squares

    def norm(off):
        return remote(nsend, nrecv.at[off - 1], ns.at[off - 1], nr.at[off - 1], (ctx, (tp + off) % 4))

    for off in (1, 2, 3):
        norm(off).start()

    for k in range(3):
        for off in OFFS:
            for axis in range(3):
                if axis > 0 or k == 2:
                    own_block(k, axis, off).wait_send()
            if k == 0:
                own_z(off).wait_send()
            for hop in OFFS:
                a_to_b(k, hop, off).wait_send()
            a_to_c(k, off).wait_send()
            b_to_c(k, off).wait_send()

    @pl.loop(0, STEPS)
    def _(t):
        for h, k in pair(t):
            for off in OFFS:
                ab_to_c(h, k, off).wait_send()
                first_back(h, k, off).wait_send()
                second_back(h, k, off).wait_send()

    for n in range(STEPS):
        for off in OFFS:
            third_back(n, off).wait_send()
    for off in (1, 2, 3):
        norm(off).wait()
    squares = squares + nrecv[0] + nrecv[1] + nrecv[2]
    mean = jnp.sum(squares, axis=1, keepdims=True) * (1.0 / (4 * HEADS * DH))
    inverse = lax.rsqrt(mean + 1e-06)
    for h in range(HEADS):
        y = attended[h] * inverse * gain_ref[h * DH : (h + 1) * DH].reshape(1, DH)
        for s in range(2):
            out_ref[s, :, h * DH : (h + 1) * DH] = y[8 * s : 8 * s + 8].astype(BF16)


def per_device(q_dec, k_dec, v_dec, ctx_k, ctx_v, lengths, gain):
    dma = pltpu.SemaphoreType.DMA
    hbm = pl.BlockSpec(memory_space=pltpu.HBM)
    scratch = [
        pltpu.VMEM((2, 8, HEADS * DH), BF16),
        pltpu.VMEM((2, 8, HEADS * DH), BF16),
        pltpu.VMEM((2, 8, HEADS * DH), BF16),
        pltpu.VMEM((2, 256, HEADS * DH), BF16),
        pltpu.VMEM((2, 256, HEADS * DH), BF16),
        pltpu.SMEM((2,), jnp.int32),
        pltpu.VMEM((HEADS * DH,), F32),
        pltpu.VMEM((HEADS, 4, 4, 4, 16, DH), BF16),
        pltpu.VMEM((HEADS, 4, 272, DH), BF16),
        pltpu.VMEM((HEADS, 3, 272, DH), BF16),
        pltpu.VMEM((HEADS, 4, 80, DH), BF16),
        pltpu.VMEM((HEADS, 3, 80, DH), BF16),
        pltpu.VMEM((STEPS, 4, 48, DH), BF16),
        pltpu.VMEM((STEPS, 3, 48, DH), BF16),
        pltpu.VMEM((HEADS, 16, DH), F32),
        pltpu.VMEM((16, DH), F32),
        pltpu.VMEM((3, 16, DH), F32),
        pltpu.VMEM((HEADS, 2, DH, 256), BF16),
        pltpu.VMEM((2, 16, HEADS * DH), BF16),
        pltpu.VMEM((HEADS, 2, 8, DH, DH), F32),
        pltpu.VMEM((2, 272, DH), F32),
        dma((7,)),
        dma((3, 3, 3)), dma((3, 3, 3)), dma((3, 3, 3)), dma((3, 3, 3)), dma((3, 2, 3)), dma((3, 2, 3)),
        dma((HEADS, 3)), dma((HEADS, 3)), dma((HEADS, 3)), dma((HEADS, 3)),
        dma((HEADS, 3)), dma((HEADS, 3)), dma((HEADS, 3)), dma((HEADS, 3)),
        dma((3,)), dma((3,)),
    ]
    return pl.pallas_call(
        kernel,
        out_shape=jax.ShapeDtypeStruct(q_dec.shape, BF16),
        in_specs=[hbm] * 7,
        out_specs=pl.BlockSpec(memory_space=pltpu.VMEM),
        scratch_shapes=scratch,
        compiler_params=pltpu.CompilerParams(
            collective_id=0, has_side_effects=True, vmem_limit_bytes=62 << 20
        ),
        cost_estimate=pl.CostEstimate(flops=1_400_000_000, bytes_accessed=8_000_000, transcendentals=2_700_000),
        name="block_attention",
    )(q_dec, k_dec, v_dec, ctx_k, ctx_v, lengths, gain)


def solution(mesh):
    return jax.shard_map(
        per_device,
        mesh=mesh,
        in_specs=(
            P(None, "ctx", "tp"),
            P(None, "ctx", "tp"),
            P(None, "ctx", "tp"),
            P(None, "ctx", "tp"),
            P(None, "ctx", "tp"),
            P(),
            P("tp"),
        ),
        out_specs=P(None, "ctx", "tp"),
        check_vma=False,
    )
```

```python
import functools
import math

import jax
import jax.numpy as jnp
from jax import lax
from jax.experimental import pallas as pl
from jax.experimental.pallas import tpu as pltpu
from jax.sharding import PartitionSpec as P

MESH = pl.DeviceIdType.MESH
DH = 128
HEADS = 10
CHUNKS = ((0, 4), (4, 4), (8, 2))
ORDER = (("z", "y", "x"), ("z", "x", "y"), ("x", "y", "z"))
STRIDE = {"z": 16, "y": 4, "x": 1}
F32 = jnp.float32
BF16 = jnp.bfloat16
NT = (((1,), (1,)), ((), ()))
OFFS = (1, 3, 2)
FAR = (2, 1, 3)
STEPS = 5
ATTEND = (0, 4, 3, 2, 1)


def kernel(
    q_hbm, kd_hbm, vd_hbm, ck_hbm, cv_hbm, len_hbm, gain_hbm, out_ref,
    q_ref, kd_ref, vd_ref, kbuf, vbuf, len_ref, gain_ref,
    qbuf, s1, r1, s2, r2, s3, r3, attended, nsend, nrecv, vt, kdp, vdb, bias,
    insem, g0s, g0r, g1s, g1r, g2s, g2r, g3s, g3r, r1s, r1r, r2s, r2r, r3s, r3r, ns, nr,
):
    ctx = lax.axis_index("ctx")
    tp = lax.axis_index("tp")
    loads = [
        pltpu.make_async_copy(src, dst, insem.at[i])
        for i, (src, dst) in enumerate((
            (q_hbm, q_ref), (kd_hbm, kd_ref), (vd_hbm, vd_ref), (ck_hbm, kbuf), (cv_hbm, vbuf), (len_hbm, len_ref), (gain_hbm, gain_ref),
        ))
    ]
    def along(stride, off):
        here = (ctx // stride) % 4
        return (ctx + ((here + off) % 4 - here) * stride, tp)

    loads[0].start()
    barrier = pltpu.get_barrier_semaphore()
    for off in (2, 1, 3):
        for name in "zyx":
            pl.semaphore_signal(barrier, inc=1, device_id=along(STRIDE[name], off), device_id_type=MESH)
        pl.semaphore_signal(barrier, inc=1, device_id=(ctx, (tp + off) % 4), device_id_type=MESH)

    for load in loads[1:]:
        load.start()

    loads[0].wait()
    own = q_ref[...].astype(F32).reshape(16, HEADS * DH).astype(BF16)
    for h in range(HEADS):
        qbuf[h, 0, 0, 0] = own[:, h * DH : (h + 1) * DH]

    pl.semaphore_wait(barrier, 12)

    def remote(src, dst, send, recv, target):
        return pltpu.make_async_remote_copy(
            src_ref=src, dst_ref=dst, send_sem=send, recv_sem=recv, device_id=target, device_id_type=MESH
        )

    def heads(k):
        return pl.ds(CHUNKS[k][0], CHUNKS[k][1])

    def own_z(off):
        both = pl.ds(0, 8)
        return remote(
            qbuf.at[both, 0, 0, 0], qbuf.at[both, 0, 0, off],
            g0s.at[0, 0, off - 1], g0r.at[0, 0, off - 1], along(STRIDE["z"], off),
        )

    def own_block(k, axis, off):
        spot = [0, 0, 0]
        spot[2 - axis] = off
        return remote(
            qbuf.at[heads(k), 0, 0, 0], qbuf.at[heads(k), spot[0], spot[1], spot[2]],
            g0s.at[k, axis, off - 1], g0r.at[k, axis, off - 1], along(STRIDE[ORDER[k][axis]], off),
        )

    def a_to_b(k, hop, off):
        return remote(
            qbuf.at[heads(k), 0, 0, hop], qbuf.at[heads(k), 0, off, hop],
            g1s.at[k, hop - 1, off - 1], g1r.at[k, hop - 1, off - 1], along(STRIDE[ORDER[k][1]], off),
        )

    def a_to_c(k, off):
        return remote(
            qbuf.at[heads(k), 0, 0, pl.ds(1, 3)], qbuf.at[heads(k), off, 0, pl.ds(1, 3)],
            g2s.at[k, 0, off - 1], g2r.at[k, 0, off - 1], along(STRIDE[ORDER[k][2]], off),
        )

    def b_to_c(k, off):
        return remote(
            qbuf.at[heads(k), 0, pl.ds(1, 3), 0], qbuf.at[heads(k), off, pl.ds(1, 3), 0],
            g2s.at[k, 1, off - 1], g2r.at[k, 1, off - 1], along(STRIDE[ORDER[k][2]], off),
        )

    def ab_to_c(h, k, off):
        return remote(
            qbuf.at[h, 0, pl.ds(1, 3), pl.ds(1, 3)], qbuf.at[h, off, pl.ds(1, 3), pl.ds(1, 3)],
            g3s.at[h, off - 1], g3r.at[h, off - 1], along(stride_c(k), off),
        )

    def pair(n):
        z = n // 4
        return ((8 * z + (1 - z) * n, 2 * z), (9 * z + (1 - z) * (4 + n), 1 + z))

    def stride_a(k):
        return 16 - 15 * (k * (k - 1) // 2)

    def stride_b(k):
        return 4 - 3 * (k * (2 - k))

    def stride_c(k):
        return 1 + 3 * k + 9 * (k * (k - 1) // 2)

    for off in FAR:
        own_z(off).start()
    for off in FAR:
        own_block(2, 0, off).start()
    for axis in (1, 2):
        for k in (2, 0, 1):
            for off in FAR:
                own_block(k, axis, off).start()

    for load in loads[1:]:
        load.wait()
    row = lax.broadcasted_iota(jnp.int32, (256, DH), 0)
    dec_row = lax.broadcasted_iota(jnp.int32, (16, DH), 0)
    for s in range(2):
        limit = len_ref[s] - ctx * 256
        bias[s, 0:256] = jnp.where(row < limit, 0.0, -jnp.inf).astype(F32)
        bias[s, 256:272] = jnp.where(dec_row < 8, 0.0, -jnp.inf).astype(F32)
        pad = jnp.zeros((8, HEADS * DH), F32)
        kdp[s] = jnp.concatenate([kd_ref[s].astype(F32), pad], axis=0).astype(BF16)
        vpad = jnp.concatenate([vd_ref[s].astype(F32), jnp.zeros((DH - 8, HEADS * DH), F32)], axis=0)
        for h in range(HEADS):
            turned_values = vpad[:, h * DH : (h + 1) * DH].T
            for j in range(8):
                vdb[h, s, j] = jnp.broadcast_to(turned_values[:, j : j + 1], (DH, DH))

    for hop in OFFS:
        for k in (2, 0, 1):
            if k == 0:
                own_z(hop).wait_recv()
            if k == 2:
                own_block(k, 0, hop).wait_recv()
            for off in FAR:
                a_to_b(k, hop, off).start()
    for k in (2, 0, 1):
        for off in FAR:
            a_to_c(k, off).start()
        for off in OFFS:
            own_block(k, 1, off).wait_recv()
        for off in FAR:
            b_to_c(k, off).start()
    for k in (2, 0, 1):
        for hop in OFFS:
            for off in OFFS:
                a_to_b(k, hop, off).wait_recv()
    for n in ATTEND:
        for h, k in pair(n):
            for off in FAR:
                ab_to_c(h, k, off).start()

    @pl.loop(0, HEADS)
    def _(h):
        lanes = pl.ds(pl.multiple_of(h * DH, DH), DH)
        for s in range(2):
            vt[h, s] = vbuf[s, :, lanes].astype(F32).T.astype(BF16)

    def first_back(h, k, off):
        return remote(s1.at[h, off], r1.at[h, off - 1], r1s.at[h, off - 1], r1r.at[h, off - 1], along(stride_c(k), 4 - off))

    def second_back(h, k, off):
        return remote(s2.at[h, off], r2.at[h, off - 1], r2s.at[h, off - 1], r2r.at[h, off - 1], along(stride_b(k), 4 - off))

    def third_back(n, off):
        k = 2 * (n // 4)
        return remote(s3.at[n, off], r3.at[n, off - 1], r3s.at[n, off - 1], r3r.at[n, off - 1], along(stride_a(k), 4 - off))

    scale = math.log2(math.e) / math.sqrt(DH)

    def split(*lses):
        rows = []
        for lse in lses:
            high = lse.astype(BF16).astype(F32)
            middle = (lse - high).astype(BF16).astype(F32)
            rows += [high, middle, lse - high - middle]
        rows.append(jnp.zeros((16 - 6 * len(lses), DH), F32))
        return jnp.concatenate(rows, axis=0).astype(BF16)

    def join(block, i=0):
        rows = block.astype(F32)[6 * i : 6 * i + 6]
        return rows[0:2] + rows[2:4] + rows[4:6]

    def attend(h, offs):
        lanes = pl.ds(pl.multiple_of(h * DH, DH), DH)
        rows = [qbuf[h, off].reshape(16, 16, DH).astype(F32) for off in offs]
        lse = []
        for s in range(2):
            q = jnp.concatenate([x[:, 8 * s : 8 * s + 8, :].reshape(DH, DH) for x in rows], axis=0).astype(BF16)
            edge = jnp.concatenate([bias[s]] * len(offs), axis=1)
            x0 = lax.dot_general(kbuf[s, :, lanes], q, NT, preferred_element_type=F32) * scale + edge[0:256]
            x1 = lax.dot_general(kdp[s, :, lanes], q, NT, preferred_element_type=F32) * scale + edge[256:272]
            peak = jnp.maximum(jnp.max(x0, axis=0, keepdims=True), jnp.max(x1, axis=0, keepdims=True))
            w0 = jnp.exp2(x0 - peak)
            w1 = jnp.exp2(x1 - peak)
            total = jnp.sum(w0, axis=0, keepdims=True) + jnp.sum(w1, axis=0, keepdims=True)
            numer = jnp.dot(vt[h, s], w0.astype(BF16), preferred_element_type=F32)
            w1 = w1.astype(BF16).astype(F32)
            block = []
            for i in range(len(offs)):
                own_part = vdb[h, s, 0] * w1[0:1, DH * i : DH * i + DH]
                for j in range(1, 8):
                    own_part += vdb[h, s, j] * w1[j : j + 1, DH * i : DH * i + DH]
                block.append(own_part)
            numer += jnp.concatenate(block, axis=1)
            part = (numer * (1.0 / total)).astype(BF16)
            lse.append(peak + jnp.log2(total))
            for i, off in enumerate(offs):
                s1[h, off, DH * s : DH * s + DH] = part[:, DH * i : DH * i + DH]
        for i, off in enumerate(offs):
            s1[h, off, 256:272] = split(jnp.concatenate([x[:, DH * i : DH * i + DH] for x in lse], axis=0))

    def merge(parts):
        peak = functools.reduce(jnp.maximum, parts)
        weights = [jnp.exp2(part - peak) for part in parts]
        total = functools.reduce(jnp.add, weights)
        inverse = 1.0 / total
        return [w * inverse for w in weights], peak + jnp.log2(total)

    def shifted(rows, lanes):
        return pltpu.roll(rows, DH - lanes, 1) if lanes else rows

    def turned(factors):
        return jnp.concatenate(factors + [jnp.zeros((DH - 8, DH), F32)], axis=0).T

    def merge_first(*pairs):
        todo = [entry for n in pairs for entry in pair(n)]
        for h, k in todo:
            for off in OFFS:
                first_back(h, k, off).wait_recv()
        results = []
        for h, k in todo:
            parts = [s1.at[h, 0]] + [r1.at[h, off - 1] for off in (1, 2, 3)]
            factors, lse = merge([join(part[256:272]) for part in parts])
            rows = []
            for s in range(2):
                acc = parts[0][DH * s : DH * s + DH].astype(F32) * factors[0][s : s + 1]
                for i in (1, 2, 3):
                    acc += parts[i][DH * s : DH * s + DH].astype(F32) * factors[i][s : s + 1]
                rows.append(acc.T.astype(BF16))
            results.append((h, rows, split(lse)))
        for h, rows, tail in results:
            for i in range(4):
                for s in range(2):
                    s2[h, i, 32 * s : 32 * s + 32] = rows[s][32 * i : 32 * i + 32]
                s2[h, i, 64:80] = tail
        for h, k in todo:
            for off in FAR:
                second_back(h, k, off).start()

    def merge_second(*pairs):
        todo = [entry for n in pairs for entry in pair(n)]
        for h, k in todo:
            for off in OFFS:
                second_back(h, k, off).wait_recv()
        results = []
        for h, k in todo:
            parts = [s2.at[h, 0]] + [r2.at[h, off - 1] for off in (1, 2, 3)]
            factors, lse = merge([shifted(join(part[64:80]), 32 * i) for i, part in enumerate(parts)])
            columns = turned(factors)[0:32]
            merged = []
            for s in range(2):
                acc = parts[0][32 * s : 32 * s + 32].astype(F32) * columns[:, s : s + 1]
                for i in (1, 2, 3):
                    acc += parts[i][32 * s : 32 * s + 32].astype(F32) * columns[:, 2 * i + s : 2 * i + s + 1]
                merged.append(acc)
            results.append((merged, lse))
        for p, n in enumerate(pairs):
            tail = split(results[2 * p][1], results[2 * p + 1][1])
            for i in range(4):
                for e in range(2):
                    rows = [m[8 * i : 8 * i + 8] for m in results[2 * p + e][0]]
                    s3[n, i, 16 * e : 16 * e + 16] = jnp.concatenate(rows, axis=0).astype(BF16)
                s3[n, i, 32:48] = tail
        for n in pairs:
            for off in FAR:
                third_back(n, off).start()

    def merge_third(*pairs):
        for n in pairs:
            for off in OFFS:
                third_back(n, off).wait_recv()
        results = []
        for n in pairs:
            parts = [s3.at[n, 0]] + [r3.at[n, off - 1] for off in (1, 2, 3)]
            for e, (h, _) in enumerate(pair(n)):
                factors, _ = merge([shifted(join(part[32:48], e), 8 * i) for i, part in enumerate(parts)])
                columns = turned(factors)[0:8]
                acc = jnp.zeros((16, DH), F32)
                for i in range(4):
                    column = jnp.concatenate([columns[:, 2 * i + s : 2 * i + s + 1] for s in range(2)], axis=0)
                    acc += parts[i][16 * e : 16 * e + 16].astype(F32) * column
                results.append((h, acc))
        for h, acc in results:
            attended[h] = acc

    @pl.loop(0, STEPS)
    def _(t):
        for h, _ in pair(t):
            attend(h, (0,))

    for k in (2, 0, 1):
        for off in OFFS:
            own_block(k, 2, off).wait_recv()
            a_to_c(k, off).wait_recv()
            b_to_c(k, off).wait_recv()

    @pl.loop(0, STEPS)
    def _(t):
        for h, k in pair((4 * t) % 5):
            for off in OFFS:
                ab_to_c(h, k, off).wait_recv()
        for h, k in pair((4 * t) % 5):
            attend(h, (1, 3, 2))
            for off in FAR:
                first_back(h, k, off).start()

    merge_first(0, 3, 2)
    merge_first(1, 4)
    merge_second(0, 3, 2)
    merge_second(1, 4)
    merge_third(0, 3, 2, 1, 4)

    squares = attended[0] * attended[0]
    for h in range(1, HEADS):
        squares += attended[h] * attended[h]
    nsend[...] = squares

    def norm(off):
        return remote(nsend, nrecv.at[off - 1], ns.at[off - 1], nr.at[off - 1], (ctx, (tp + off) % 4))

    for off in (1, 2, 3):
        norm(off).start()

    for k in range(3):
        for off in OFFS:
            for axis in range(3):
                if axis > 0 or k == 2:
                    own_block(k, axis, off).wait_send()
            if k == 0:
                own_z(off).wait_send()
            for hop in OFFS:
                a_to_b(k, hop, off).wait_send()
            a_to_c(k, off).wait_send()
            b_to_c(k, off).wait_send()

    @pl.loop(0, STEPS)
    def _(t):
        for h, k in pair(t):
            for off in OFFS:
                ab_to_c(h, k, off).wait_send()
                first_back(h, k, off).wait_send()
                second_back(h, k, off).wait_send()

    for n in range(STEPS):
        for off in OFFS:
            third_back(n, off).wait_send()
    for off in (1, 2, 3):
        norm(off).wait()
    squares = squares + nrecv[0] + nrecv[1] + nrecv[2]
    mean = jnp.sum(squares, axis=1, keepdims=True) * (1.0 / (4 * HEADS * DH))
    inverse = lax.rsqrt(mean + 1e-06)
    for h in range(HEADS):
        y = attended[h] * inverse * gain_ref[h * DH : (h + 1) * DH].reshape(1, DH)
        for s in range(2):
            out_ref[s, :, h * DH : (h + 1) * DH] = y[8 * s : 8 * s + 8].astype(BF16)


def per_device(q_dec, k_dec, v_dec, ctx_k, ctx_v, lengths, gain):
    dma = pltpu.SemaphoreType.DMA
    hbm = pl.BlockSpec(memory_space=pltpu.HBM)
    scratch = [
        pltpu.VMEM((2, 8, HEADS * DH), BF16),
        pltpu.VMEM((2, 8, HEADS * DH), BF16),
        pltpu.VMEM((2, 8, HEADS * DH), BF16),
        pltpu.VMEM((2, 256, HEADS * DH), BF16),
        pltpu.VMEM((2, 256, HEADS * DH), BF16),
        pltpu.SMEM((2,), jnp.int32),
        pltpu.VMEM((HEADS * DH,), F32),
        pltpu.VMEM((HEADS, 4, 4, 4, 16, DH), BF16),
        pltpu.VMEM((HEADS, 4, 272, DH), BF16),
        pltpu.VMEM((HEADS, 3, 272, DH), BF16),
        pltpu.VMEM((HEADS, 4, 80, DH), BF16),
        pltpu.VMEM((HEADS, 3, 80, DH), BF16),
        pltpu.VMEM((STEPS, 4, 48, DH), BF16),
        pltpu.VMEM((STEPS, 3, 48, DH), BF16),
        pltpu.VMEM((HEADS, 16, DH), F32),
        pltpu.VMEM((16, DH), F32),
        pltpu.VMEM((3, 16, DH), F32),
        pltpu.VMEM((HEADS, 2, DH, 256), BF16),
        pltpu.VMEM((2, 16, HEADS * DH), BF16),
        pltpu.VMEM((HEADS, 2, 8, DH, DH), F32),
        pltpu.VMEM((2, 272, DH), F32),
        dma((7,)),
        dma((3, 3, 3)), dma((3, 3, 3)), dma((3, 3, 3)), dma((3, 3, 3)), dma((3, 2, 3)), dma((3, 2, 3)),
        dma((HEADS, 3)), dma((HEADS, 3)), dma((HEADS, 3)), dma((HEADS, 3)),
        dma((HEADS, 3)), dma((HEADS, 3)), dma((HEADS, 3)), dma((HEADS, 3)),
        dma((3,)), dma((3,)),
    ]
    return pl.pallas_call(
        kernel,
        out_shape=jax.ShapeDtypeStruct(q_dec.shape, BF16),
        in_specs=[hbm] * 7,
        out_specs=pl.BlockSpec(memory_space=pltpu.VMEM),
        scratch_shapes=scratch,
        compiler_params=pltpu.CompilerParams(
            collective_id=0, has_side_effects=True, vmem_limit_bytes=62 << 20
        ),
        cost_estimate=pl.CostEstimate(flops=1_400_000_000, bytes_accessed=8_000_000, transcendentals=2_700_000),
        name="block_attention",
    )(q_dec, k_dec, v_dec, ctx_k, ctx_v, lengths, gain)


def solution(mesh):
    return jax.shard_map(
        per_device,
        mesh=mesh,
        in_specs=(
            P(None, "ctx", "tp"),
            P(None, "ctx", "tp"),
            P(None, "ctx", "tp"),
            P(None, "ctx", "tp"),
            P(None, "ctx", "tp"),
            P(),
            P("tp"),
        ),
        out_specs=P(None, "ctx", "tp"),
        check_vma=False,
    )
```
